256 devices in a mesh: row: 16 (over y, x), col: 16 (over z, core).
Axes of the slice: x: 4, y: 4, z: 8, core: 2. Of those that a mesh axis runs over, the one named last changes fastest.
Arguments:
- embedding: bfloat16 [1024, 1024, 256], P('row', 'col'), may hold values from -6 to 6
- counts: int32 [16, 16], P('col'), may hold values from 1 to 48, 256 in all within a row
- points: int32 [16, 16, 2, 48], P('row', 'col'), may hold values from 0 to 1023
- pe_gauss: float32 [2, 128], replicated, may hold values from -6 to 6
- point_embed: float32 [256], replicated, may hold values from -6 to 6
- mask_token: float32 [256], replicated, may hold values from -6 to 6
- sa_qkv: bfloat16 [256, 768], replicated, may hold values from -0.375 to 0.375
- sa_out: bfloat16 [256, 256], replicated, may hold values from -0.375 to 0.375
- t2i_qkv: bfloat16 [256, 384], replicated, may hold values from -0.375 to 0.375
- t2i_out: bfloat16 [128, 256], replicated, may hold values from -0.5 to 0.5
- mlp_up: bfloat16 [256, 2048], replicated, may hold values from -0.375 to 0.375
- mlp_down: bfloat16 [2048, 256], replicated, may hold values from -0.125 to 0.125
- i2t_qkv: bfloat16 [256, 384], replicated, may hold values from -0.375 to 0.375
- i2t_out: bfloat16 [128, 256], replicated, may hold values from -0.5 to 0.5
- hyper_w: bfloat16 [2, 256, 256], replicated, may hold values from -0.375 to 0.375
- ln_gains: float32 [4, 256], replicated, may hold values from 0.1 to 1.9
Outputs:
- mask_logits: bfloat16 [16, 16, 48, 4096], P('row', 'col')
- seam_blend: float32 [1024, 1024], P('row', 'col')
The draws below stay inside these ranges and needn't reach their ends.
Inputs may be any that keep to these rules, and one draw needn't show every extreme that they name: For each column index the counts of its 16 tiles sum to 256, and the largest of them is 48. `points`: slots at or past a tile's count hold coordinates that no output reads.
All inputs are finite; a program needn't handle non-finite values.
Results may differ from the reference program's by a relative error of at most 0.012.
Values may be sent and summed in bfloat16 or wider, within the bound.
A program may use at most 128 MiB of HBM per device.

```python
import math
import jax
import jax.numpy as jnp
import numpy as np
from jax import lax

D = 256
MLP = 2048
HEADS = 8
GRID = 64
SEAM = 4
DI = 128
IMG = 1024
CAP = 48
TOTAL = 256
N_ROW = 16
N_COL = 16


def place_ends(values, own_key, smallest, top_value):
    place = [jax.random.randint(jax.random.fold_in(own_key, axis), (), 0, length) for axis, length in enumerate(values.shape)]
    widest = values.shape.index(max(values.shape))
    next_to = place[:widest] + [(place[widest] + 1) % values.shape[widest]] + place[widest + 1:]
    return values.at[tuple(place)].set(smallest).at[tuple(next_to)].set(top_value)


def steps_of(stream_key, dims, cuts, smallest, largest):
    loudness = 1.0
    for position, parts in cuts:
        draws = jax.random.uniform(jax.random.fold_in(jax.random.fold_in(stream_key, 6), position), (parts,), jnp.float32, smallest / len(cuts), largest / len(cuts))
        loudness = loudness * jnp.repeat(jnp.exp(draws), dims[position] // parts).reshape((-1,) + (1,) * (len(dims) - 1 - position))
    return loudness


def profile(count, total, reach, skew):
    loads = [(1 << 20) // math.isqrt(standing ** skew) + 1 for standing in range(2, count + 1)]
    rest, given = total - reach - (count - 1), [1] * (count - 1)
    while rest > 0:
        candidates = [i for i in range(count - 1) if given[i] < reach]
        pool, budget = sum([loads[i] for i in candidates]), rest
        for i in candidates:
            addition = min(reach - given[i], max(1, budget * loads[i] // pool), rest)
            given[i] = given[i] + addition
            rest = rest - addition
    return np.array([reach] + given)


def ragged_sizes(own_key, amount, total, most, skew):
    if amount == 2:
        one = jax.random.randint(own_key, (), max(1, total - most), min(most, total - 1) + 1)
        return jnp.stack([one, total - one])
    tallies = jnp.asarray(profile(amount, total, most, skew), jnp.int32)
    twos = (amount - 1) // 2
    giver, sink = tallies[1:1 + 2 * twos:2], tallies[2:2 + 2 * twos:2]
    margin = jnp.minimum(giver - 1, most - sink)
    passed = jax.random.randint(jax.random.fold_in(own_key, 1), (twos,), 0, 1 << 20) % (margin + 1)
    tallies = tallies.at[1:1 + 2 * twos:2].set(giver - passed).at[2:2 + 2 * twos:2].set(sink + passed)
    return tallies[jax.random.permutation(jax.random.fold_in(own_key, 2), amount)]


def noise(own_key, shape, scale, reach, shards=(), kind=jnp.bfloat16):
    drawn = jax.random.normal(own_key, shape, jnp.float32) * scale
    if len(shards) > 0:
        drawn = steps_of(own_key, shape, shards, -0.22, 0.18) * drawn
    return jnp.clip(drawn, min=-reach, max=reach).astype(kind)


def setup_inputs(seed: int = 0) -> dict:
    splits = jax.random.split(jax.random.key(seed), 17)
    embedding = noise(splits[0], (N_ROW * GRID, N_COL * GRID, D), 1.0, 6.0, ((0, 16), (1, 16)))
    counts = jax.vmap(lambda own: ragged_sizes(own, N_ROW, TOTAL, CAP, 2))(jax.random.split(splits[1], N_COL)).reshape((N_COL, N_ROW)).astype(jnp.int32)
    points = place_ends(jax.random.randint(splits[2], (N_ROW, N_COL, 2, CAP), 0, IMG), jax.random.fold_in(splits[2], 1), 0, IMG - 1).astype(jnp.int32)
    pe_gauss = noise(splits[3], (2, D // 2), 1.0, 6.0, (), jnp.float32)
    point_embed = noise(splits[4], (D,), 1.0, 6.0, (), jnp.float32)
    mask_token = noise(splits[5], (D,), 1.0, 6.0, (), jnp.float32)
    sa_qkv = noise(splits[6], (D, 3 * D), D ** -0.5, 0.375)
    sa_out = noise(splits[7], (D, D), D ** -0.5, 0.375)
    t2i_qkv = noise(splits[8], (D, 3 * DI), D ** -0.5, 0.375)
    t2i_out = noise(splits[9], (DI, D), DI ** -0.5, 0.5)
    mlp_up = noise(splits[10], (D, MLP), D ** -0.5, 0.375)
    mlp_down = noise(splits[11], (MLP, D), MLP ** -0.5, 0.125)
    i2t_qkv = noise(splits[12], (D, 3 * DI), D ** -0.5, 0.375)
    i2t_out = noise(splits[13], (DI, D), DI ** -0.5, 0.5)
    hyper_w = noise(splits[14], (2, D, D), D ** -0.5, 0.375)
    ln_gains = jnp.clip(1.0 + 0.18 * jax.random.normal(splits[15], (4, D), jnp.float32), 0.1, 1.9)
    return dict(embedding=embedding, counts=counts, points=points, pe_gauss=pe_gauss, point_embed=point_embed, mask_token=mask_token, sa_qkv=sa_qkv, sa_out=sa_out, t2i_qkv=t2i_qkv, t2i_out=t2i_out, mlp_up=mlp_up, mlp_down=mlp_down, i2t_qkv=i2t_qkv, i2t_out=i2t_out, hyper_w=hyper_w, ln_gains=ln_gains)


norm_eps = 1e-05
highest = lax.Precision.HIGHEST

def layer_norm(values, norm_gain):
    row_mean = lax.optimization_barrier(jnp.mean(values, axis=-1, keepdims=True))
    centred = values - row_mean
    row_var = lax.optimization_barrier(jnp.mean(centred * centred, axis=-1, keepdims=True))
    return centred * lax.rsqrt(row_var + norm_eps) * norm_gain

def weight_dot(values, weight):
    return jnp.dot(values, weight.astype(jnp.float32), precision=highest)

def fourier(norm_x, norm_y, pe_gauss):
    phases = 2.0 * math.pi * ((2.0 * norm_x - 1.0)[:, None] * pe_gauss[0] + (2.0 * norm_y - 1.0)[:, None] * pe_gauss[1])
    return jnp.concatenate([jnp.sin(phases), jnp.cos(phases)], axis=-1)

def dense_pe(pixel_ids, grid_side, pe_gauss):
    norm_x = ((pixel_ids % grid_side).astype(jnp.float32) + 0.5) / grid_side
    norm_y = ((pixel_ids // grid_side).astype(jnp.float32) + 0.5) / grid_side
    return fourier(norm_x, norm_y, pe_gauss)

def softmax_last(scores):
    row_top = lax.optimization_barrier(jnp.max(scores, axis=-1, keepdims=True))
    exp_scores = jnp.exp(scores - row_top)
    return exp_scores / lax.optimization_barrier(jnp.sum(exp_scores, axis=-1, keepdims=True))

def token_side(points_xy, keys_pe, tile_flat, pe_gauss, point_embed, mask_token, sa_qkv, sa_out, t2i_qkv, t2i_out, mlp_up, mlp_down, i2t_qkv, hyper_w, ln_gains):
    slot_count = points_xy.shape[1]
    model_width = keys_pe.shape[1]
    pixel_count = keys_pe.shape[0]
    inner_width = t2i_qkv.shape[1] // 3
    self_width = model_width // HEADS
    head_width = inner_width // HEADS
    coords = (points_xy.astype(jnp.float32) + 0.5) / IMG
    prompt = fourier(coords[0], coords[1], pe_gauss) + point_embed
    start_tok = jnp.stack([jnp.broadcast_to(mask_token, (slot_count, model_width)), prompt], axis=1)
    self_qkv = weight_dot(start_tok, sa_qkv).reshape(slot_count, 2, 3, HEADS, self_width)
    self_score = jnp.einsum('cqhd,ckhd->chqk', self_qkv[:, :, 0], self_qkv[:, :, 1], precision=highest) / math.sqrt(self_width)
    self_out = jnp.einsum('chqk,ckhd->cqhd', softmax_last(self_score), self_qkv[:, :, 2], precision=highest)
    queries = layer_norm(weight_dot(self_out.reshape(slot_count, 2, model_width), sa_out), ln_gains[0])
    cross_q = weight_dot(queries + start_tok, t2i_qkv[:, :inner_width]).astype(jnp.bfloat16)
    cross_k = jnp.dot(keys_pe, t2i_qkv[:, inner_width:2 * inner_width], preferred_element_type=jnp.float32).astype(jnp.bfloat16)
    cross_v = jnp.dot(tile_flat, t2i_qkv[:, 2 * inner_width:], preferred_element_type=jnp.float32).astype(jnp.bfloat16)
    cross_score = jnp.einsum('cqhd,phd->chqp', cross_q.reshape(slot_count, 2, HEADS, head_width).astype(jnp.float32), cross_k.reshape(pixel_count, HEADS, head_width).astype(jnp.float32), precision=highest) / math.sqrt(head_width)
    cross_prob = softmax_last(cross_score).astype(jnp.bfloat16)
    cross_out = jnp.einsum('chqp,phd->cqhd', cross_prob.astype(jnp.float32), cross_v.reshape(pixel_count, HEADS, head_width).astype(jnp.float32), precision=highest)
    queries = layer_norm(queries + weight_dot(cross_out.reshape(slot_count, 2, inner_width), t2i_out), ln_gains[1])
    hidden = jax.nn.relu(weight_dot(queries, mlp_up))
    queries = layer_norm(queries + weight_dot(hidden, mlp_down), ln_gains[2])
    back_k = weight_dot(queries + start_tok, i2t_qkv[:, inner_width:2 * inner_width]).astype(jnp.bfloat16)
    back_v = weight_dot(queries, i2t_qkv[:, 2 * inner_width:]).astype(jnp.bfloat16)
    kv_rows = jnp.concatenate([back_k, back_v], axis=1)
    hyper_rows = weight_dot(jax.nn.relu(weight_dot(queries[:, 0], hyper_w[0])), hyper_w[1]).astype(jnp.bfloat16)
    return (kv_rows, hyper_rows)

def image_side(tile_rows, query_rows, kv_rows, hyper_rows, out_weight, norm_gain):
    batch_rows, pix_rows, inner_width = query_rows.shape
    head_width = inner_width // HEADS
    head_query = query_rows.reshape(batch_rows, pix_rows, HEADS, head_width).astype(jnp.float32)
    head_keys = kv_rows[:, 0:2].reshape(batch_rows, 2, HEADS, head_width).astype(jnp.float32)
    values = kv_rows[:, 2:4].reshape(batch_rows, 2, HEADS, head_width).astype(jnp.float32)
    scores = jnp.einsum('bphd,bkhd->bphk', head_query, head_keys, precision=highest) / math.sqrt(head_width)
    attention = softmax_last(scores)
    mixture = jnp.einsum('bphk,bkhd->bphd', attention, values, precision=highest)
    mixture = mixture.reshape(batch_rows, pix_rows, inner_width).astype(jnp.bfloat16)
    update = jnp.einsum('bpi,id->bpd', mixture.astype(jnp.float32), out_weight.astype(jnp.float32), precision=highest)
    normed = layer_norm(tile_rows.astype(jnp.float32) + update, norm_gain)
    model_width = normed.shape[-1]
    return (lax.optimization_barrier(jnp.sum(normed * hyper_rows.astype(jnp.float32)[:, None, :], axis=-1)) / math.sqrt(model_width)).astype(jnp.bfloat16)

def reference(embedding, counts, points, pe_gauss, point_embed, mask_token, sa_qkv, sa_out, t2i_qkv, t2i_out, mlp_up, mlp_down, i2t_qkv, i2t_out, hyper_w, ln_gains):
    grid_side = GRID
    pixel_count = grid_side * grid_side
    row_count = N_ROW
    col_count = N_COL
    tile_total = row_count * col_count
    tiles = embedding.reshape(row_count, grid_side, col_count, grid_side, D).transpose(0, 2, 1, 3, 4).reshape(tile_total, pixel_count, D)
    tile_points = points.reshape(tile_total, 2, CAP)
    image_pe = dense_pe(jnp.arange(pixel_count, dtype=jnp.int32), grid_side, pe_gauss)

    def per_tile(tile_item):
        tile_flat, points_xy = tile_item
        keys_pe = (tile_flat.astype(jnp.float32) + image_pe).astype(jnp.bfloat16)
        kv_rows, hyper_rows = token_side(points_xy, keys_pe, tile_flat, pe_gauss, point_embed, mask_token, sa_qkv, sa_out, t2i_qkv, t2i_out, mlp_up, mlp_down, i2t_qkv, hyper_w, ln_gains)
        image_query = jnp.dot(keys_pe, i2t_qkv[:, :DI], preferred_element_type=jnp.float32).astype(jnp.bfloat16)
        return (kv_rows, hyper_rows, image_query)
    kv_all, hyper_all, query_all = lax.map(per_tile, (tiles, tile_points))
    live_flat = counts.T.reshape(tile_total).astype(jnp.int32)
    count_ends = jnp.cumsum(live_flat).astype(jnp.int32)
    count_starts = (count_ends - live_flat).astype(jnp.int32)
    live_total = col_count * TOTAL
    packed_order = jnp.arange(live_total, dtype=jnp.int32)
    tile_of = lax.optimization_barrier(jnp.sum((packed_order[:, None] >= count_ends[None, :]).astype(jnp.int32), axis=1)).astype(jnp.int32)
    slot_of = (packed_order - count_starts[tile_of]).astype(jnp.int32)

    def per_block(packed_ids):
        tile_ids, slot_ids = packed_ids
        return image_side(tiles[tile_ids], query_all[tile_ids], kv_all[tile_ids, slot_ids], hyper_all[tile_ids, slot_ids], i2t_out, ln_gains[3])
    logits = lax.map(per_block, (tile_of.reshape(-1, row_count), slot_of.reshape(-1, row_count))).reshape(live_total, pixel_count)
    mask_logits = jnp.zeros((tile_total, CAP, pixel_count), jnp.bfloat16).at[tile_of, slot_of].set(logits)
    keep_slot = jnp.arange(CAP, dtype=jnp.int32)[None, :, None] < live_flat[:, None, None]
    coverage = lax.optimization_barrier(jnp.sum(jnp.where(keep_slot, jax.nn.sigmoid(mask_logits.astype(jnp.float32)), jnp.float32(0.0)), axis=1))
    coverage = coverage.reshape(row_count, col_count, grid_side, grid_side).transpose(0, 2, 1, 3).reshape(row_count * grid_side, col_count * grid_side)
    padded = jnp.pad(coverage, ((0, 0), (SEAM, SEAM)))
    width_all = col_count * grid_side
    blended = jnp.zeros_like(coverage)
    for offset in range(-SEAM, SEAM + 1):
        factor = (SEAM + 1 - abs(offset)) / (SEAM + 1) ** 2
        blended = blended + factor * padded[:, SEAM + offset:SEAM + offset + width_all]
    return (mask_logits.reshape(row_count, col_count, CAP, pixel_count), blended)
```

```python
import functools
import math

import jax
import jax.numpy as jnp
import numpy as np
from jax import lax
from jax.experimental import pallas as pl
from jax.experimental.pallas import tpu as pltpu
from jax.sharding import PartitionSpec as P

HEADS = 8
SEAM = 4
IMG = 1024
EPS = 1e-05
F32 = jnp.float32
BF16 = jnp.bfloat16
LANES = 128
CHUNK = 512
GROUP = 16


def turn_polynomials():
    z = np.linspace(0.0, 0.25, 4001)[1:]
    r = np.sqrt(z)
    fit = np.polynomial.chebyshev.Chebyshev.fit
    power = lambda c: [float(v) for v in c.convert(kind=np.polynomial.Polynomial, domain=[-1, 1]).coef]
    return (
        power(fit(z, np.sin(2 * math.pi * r) / r, 8, domain=[0.0, 0.25])),
        power(fit(z, np.cos(2 * math.pi * r), 8, domain=[0.0, 0.25])),
    )


SIN_COEF, COS_COEF = turn_polynomials()


def sin_cos_turns(turns):
    r = turns - jnp.floor(turns + 0.5)
    z = r * r
    s = jnp.full_like(z, SIN_COEF[-1])
    c = jnp.full_like(z, COS_COEF[-1])
    for a, b in zip(SIN_COEF[-2::-1], COS_COEF[-2::-1]):
        s = s * z + a
        c = c * z + b
    return s * r, c


def dot(a, b):
    return lax.dot_general(a, b, (((1,), (0,)), ((), ())), preferred_element_type=F32)


def dot_t(a, b):
    return lax.dot_general(a, b, (((1,), (1,)), ((), ())), preferred_element_type=F32)


def halves(values):
    high = values.astype(BF16)
    return high, (values - high.astype(F32)).astype(BF16)


def weight_dot(values, weight):
    rows = values.shape[0]
    both = dot(jnp.concatenate(halves(values), axis=0), weight)
    return both[:rows] + both[rows:]


def layer_norm(values, gain):
    centred = values - jnp.mean(values, axis=-1, keepdims=True)
    var = jnp.mean(centred * centred, axis=-1, keepdims=True)
    return centred * lax.rsqrt(var + EPS) * gain


def rounded(values):
    return values.astype(BF16).astype(F32)


def by_head(values):
    lane = lax.broadcasted_iota(jnp.int32, values.shape, 1) // (values.shape[1] // HEADS)
    return jnp.concatenate([jnp.where(lane == h, values, 0.0) for h in range(HEADS)], axis=0)


def centred_rows(values):
    return values - jnp.mean(values, axis=-1, keepdims=True)


def as_column(row):
    n = row.shape[1]
    i = lax.broadcasted_iota(jnp.int32, (n, n), 0)
    j = lax.broadcasted_iota(jnp.int32, (n, n), 1)
    return jnp.sum(jnp.where(i == j, jnp.broadcast_to(row, (n, n)), 0.0), axis=1, keepdims=True)


def tile_kernel(
    counts_ref,
    emb_ref,
    points_ref,
    gauss_ref,
    prompt_ref,
    mask_ref,
    sa_qkv_ref,
    sa_out_ref,
    t2i_ref,
    t2i_out_ref,
    up_ref,
    down_ref,
    i2t_ref,
    i2t_out_ref,
    hyper_ref,
    gains_ref,
    logits_ref,
    cov_ref,
    keys_ref,
    sq_ref,
    table_ref,
    score_ref,
    aq_ref,
    top_ref,
    sum_ref,
    acc_ref,
    gap_ref,
    row_ref,
    coef_ref,
    t_ref,
    r_ref,
):
    cells, width = emb_ref.shape
    slots = points_ref.shape[1]
    tokens = 2 * slots
    half = width // 2
    inner = t2i_ref.shape[1] // 3
    side = math.isqrt(cells)
    chunks = cells // CHUNK
    count = counts_ref[0, lax.axis_index("row")]

    steps = (2.0 * (lax.broadcasted_iota(jnp.int32, (side, half), 0).astype(F32) + 0.5)) / side - 1.0
    sin_x, cos_x = sin_cos_turns(steps * gauss_ref[0:1, :])
    sin_y, cos_y = sin_cos_turns(steps * gauss_ref[1:2, :])
    table_ref[0] = sin_y
    table_ref[1] = cos_y

    def cell_body(y, carry):
        at = pl.multiple_of(y * side, side)
        e = emb_ref[pl.ds(at, side), :].astype(F32)
        sy = table_ref[0, pl.ds(y, 1), :]
        cy = table_ref[1, pl.ds(y, 1), :]
        e1, e2 = e[:, :half], e[:, half:]
        keys_ref[pl.ds(at, side), :half] = (e1 + (sin_x * cy + cos_x * sy)).astype(BF16)
        keys_ref[pl.ds(at, side), half:] = (e2 + (cos_x * cy - sin_x * sy)).astype(BF16)
        high, low = halves(e1 * e1 + e2 * e2)
        sq_ref[pl.ds(at, side), :half] = high
        sq_ref[pl.ds(at, side), half:] = low
        return carry

    lax.fori_loop(0, side, cell_body, 0)

    coords = (2.0 * (points_ref[...].astype(F32) + 0.5)) / IMG - 1.0
    turns = as_column(coords[0:1, :]) * gauss_ref[0:1, :] + as_column(coords[1:2, :]) * gauss_ref[1:2, :]
    sin_p, cos_p = sin_cos_turns(turns)
    prompt = jnp.concatenate([sin_p, cos_p], axis=1) + prompt_ref[...]
    start = jnp.concatenate([jnp.broadcast_to(mask_ref[...], (slots, width)), prompt], axis=0)
    qkv = weight_dot(start, sa_qkv_ref[...])
    q, k, v = qkv[:, :width], qkv[:, width : 2 * width], qkv[:, 2 * width :]
    k_gap = k[slots:] - k[:slots]
    v_gap = v[slots:] - v[:slots]
    self_width = width // HEADS
    i = lax.broadcasted_iota(jnp.int32, (width, width), 0) // self_width
    j = lax.broadcasted_iota(jnp.int32, (width, width), 1) // self_width
    same = jnp.where(i == j, 1.0, 0.0).astype(BF16)
    gap = weight_dot(q * jnp.concatenate([k_gap, k_gap], axis=0), same) / math.sqrt(self_width)
    second = jax.nn.sigmoid(gap)
    joined = jnp.concatenate([v[:slots], v[:slots]], axis=0) + second * jnp.concatenate([v_gap, v_gap], axis=0)
    queries = layer_norm(weight_dot(joined, sa_out_ref[...]), gains_ref[0:1, :])
    cross_q = rounded(weight_dot(queries + start, t2i_ref[:, :inner]))
    scale = math.log2(math.e) / math.sqrt(inner // HEADS)
    aq_ref[...] = (dot_t(by_head(cross_q).astype(BF16), t2i_ref[:, inner : 2 * inner]) * scale).astype(BF16)

    top_ref[...] = jnp.full(top_ref.shape, -jnp.inf, F32)

    def score_body(c, carry):
        at = pl.multiple_of(c * CHUNK, CHUNK)
        s = dot_t(aq_ref[...], keys_ref[pl.ds(at, CHUNK), :])
        score_ref[:, pl.ds(at, CHUNK)] = s
        top = top_ref[...]
        for k0 in range(0, CHUNK, LANES):
            top = jnp.maximum(top, s[:, k0 : k0 + LANES])
        top_ref[...] = top
        return carry

    lax.fori_loop(0, chunks, score_body, 0)
    top_ref[...] = jnp.broadcast_to(jnp.max(top_ref[...], axis=1, keepdims=True), top_ref.shape)
    sum_ref[...] = jnp.zeros_like(sum_ref)
    acc_ref[...] = jnp.zeros_like(acc_ref)

    def prob_body(c, carry):
        at = pl.multiple_of(c * CHUNK, CHUNK)
        top = top_ref[...]
        total = sum_ref[...]
        parts = []
        for k0 in range(0, CHUNK, LANES):
            p = jnp.exp2(score_ref[:, pl.ds(pl.multiple_of(at + k0, LANES), LANES)] - top)
            total = total + p
            parts.append(p.astype(BF16))
        sum_ref[...] = total
        acc_ref[...] += dot(jnp.concatenate(parts, axis=1), emb_ref[pl.ds(at, CHUNK), :])
        return carry

    lax.fori_loop(0, chunks, prob_body, 0)
    mean_cell = acc_ref[...] / jnp.sum(sum_ref[...], axis=1, keepdims=True)
    head_out = dot(mean_cell.astype(BF16), t2i_ref[:, 2 * inner :])
    lane = lax.broadcasted_iota(jnp.int32, (tokens, inner), 1) // (inner // HEADS)
    cross_out = jnp.zeros((tokens, inner), F32)
    for h in range(HEADS):
        cross_out = jnp.where(lane == h, head_out[h * tokens : (h + 1) * tokens], cross_out)

    queries = layer_norm(queries + weight_dot(cross_out, t2i_out_ref[...]), gains_ref[1:2, :])
    hidden = jnp.maximum(weight_dot(queries, up_ref[...]), 0.0)
    queries = layer_norm(queries + weight_dot(hidden, down_ref[...]), gains_ref[2:3, :])
    back_k = rounded(weight_dot(queries + start, i2t_ref[:, inner : 2 * inner]))
    back_v = rounded(weight_dot(queries, i2t_ref[:, 2 * inner :]))
    hyper = rounded(weight_dot(jnp.maximum(weight_dot(queries[:slots], hyper_ref[0]), 0.0), hyper_ref[1]))

    key_gap = back_k[:slots] - back_k[slots:]
    gap_scale = 0.5 / math.sqrt(inner // HEADS)
    gap_ref[...] = (dot_t(by_head(key_gap).astype(BF16), i2t_ref[:, :inner]) * gap_scale).astype(BF16)
    spread = 0.5 * (back_v[:slots] - back_v[slots:])
    middle = 0.5 * (back_v[:slots] + back_v[slots:])
    u = rounded(centred_rows(dot(by_head(spread).astype(BF16), i2t_out_ref[...])))
    b = rounded(centred_rows(weight_dot(middle, i2t_out_ref[...])))
    g = rounded(centred_rows(hyper * gains_ref[3:4, :]))
    heads = HEADS * slots
    row_ref[:heads, :] = (2.0 * u).astype(BF16)
    row_ref[heads : heads + slots, :] = (2.0 * b).astype(BF16)
    row_ref[heads + slots : heads + 2 * slots, :] = g.astype(BF16)
    row_ref[heads + 2 * slots :, :] = jnp.ones((row_ref.shape[0] - heads - 2 * slots, width), BF16)

    def product(left, right, factor):
        value = jnp.sum(left * right, axis=1, keepdims=True) * factor
        return jnp.broadcast_to(value, (slots, LANES))

    us = [u[h * slots : (h + 1) * slots] for h in range(HEADS)]
    n = 0
    for h in range(HEADS):
        for h2 in range(h + 1):
            coef_ref[n] = product(us[h], us[h2], 1.0 if h == h2 else 2.0)
            n += 1
    for h in range(HEADS):
        coef_ref[n + h] = product(us[h], b, 2.0)
        coef_ref[n + HEADS + h] = product(us[h], g, 1.0)
    n += 2 * HEADS
    coef_ref[n] = product(b, b, 1.0)
    coef_ref[n + 1] = product(b, g, 1.0)

    ones = jnp.ones((GROUP, width), BF16)

    def image_body(c, carry):
        at = pl.multiple_of(c * CHUNK, CHUNK)
        t_ref[...] = jnp.tanh(dot_t(gap_ref[...], keys_ref[pl.ds(at, CHUNK), :]))
        r_ref[...] = dot_t(row_ref[...], emb_ref[pl.ds(at, CHUNK), :])
        squares = dot_t(ones, sq_ref[pl.ds(at, CHUNK), :])
        for k0 in range(0, CHUNK, LANES):
            lanes = slice(k0, k0 + LANES)
            sums = r_ref[heads + 2 * slots :, lanes]
            own = squares[:, lanes] - sums * sums * (1.0 / width)
            cover = jnp.zeros((8, LANES), F32)
            for s0 in range(0, slots, GROUP):
                rows = slice(s0, s0 + GROUP)
                ts = [t_ref[h * slots + s0 : h * slots + s0 + GROUP, lanes] for h in range(HEADS)]
                var = own + r_ref[heads + s0 : heads + s0 + GROUP, lanes] + coef_ref[n, rows]
                out = r_ref[heads + slots + s0 : heads + slots + s0 + GROUP, lanes] + coef_ref[n + 1, rows]
                m = 0
                for h in range(HEADS):
                    line = r_ref[h * slots + s0 : h * slots + s0 + GROUP, lanes] + coef_ref[n - 2 * HEADS + h, rows]
                    for h2 in range(h + 1):
                        line = line + ts[h2] * coef_ref[m, rows]
                        m += 1
                    var = var + ts[h] * line
                    out = out + ts[h] * coef_ref[n - HEADS + h, rows]
                var = jnp.maximum(var, 0.0)
                logit = (out * lax.rsqrt(var + EPS * width)).astype(BF16)
                live = lax.broadcasted_iota(jnp.int32, (GROUP, LANES), 0) + s0 < count
                masked = jnp.where(live, logit.astype(F32), 0.0)
                logits_ref[rows, pl.ds(pl.multiple_of(at + k0, LANES), LANES)] = masked.astype(BF16)
                sig = jnp.where(live, jax.nn.sigmoid(masked), 0.0)
                cover = cover + (sig[:8] + sig[8:])
            cov_ref[pl.ds(c * (CHUNK // LANES) + k0 // LANES, 1), :] = jnp.sum(cover, axis=0, keepdims=True)
        return carry

    lax.fori_loop(0, chunks, image_body, 0)


def seam_kernel(n, cov_ref, out_ref, left_ref, right_ref, send_sem, recv_sem):
    me = lax.axis_index("col")
    side = out_ref.shape[0]
    has_left, has_right = me > 0, me < n - 1
    barrier = pltpu.get_barrier_semaphore()
    mesh_id = pl.DeviceIdType.MESH

    def to_left():
        return pltpu.make_async_remote_copy(
            src_ref=cov_ref,
            dst_ref=right_ref,
            send_sem=send_sem.at[0],
            recv_sem=recv_sem.at[0],
            device_id={"col": me - 1},
            device_id_type=mesh_id,
        )

    def to_right():
        return pltpu.make_async_remote_copy(
            src_ref=cov_ref,
            dst_ref=left_ref,
            send_sem=send_sem.at[1],
            recv_sem=recv_sem.at[1],
            device_id={"col": me + 1},
            device_id_type=mesh_id,
        )

    @pl.when(has_left)
    def _():
        pl.semaphore_signal(barrier, inc=1, device_id={"col": me - 1}, device_id_type=mesh_id)

    @pl.when(has_right)
    def _():
        pl.semaphore_signal(barrier, inc=1, device_id={"col": me + 1}, device_id_type=mesh_id)

    pl.semaphore_wait(barrier, has_left.astype(jnp.int32) + has_right.astype(jnp.int32))

    @pl.when(has_left)
    def _():
        to_left().start()

    @pl.when(has_right)
    def _():
        to_right().start()

    cov = cov_ref[...]
    x = lax.broadcasted_iota(jnp.int32, cov.shape, 1) % side
    total = (SEAM + 1.0) * cov
    for d in range(1, SEAM + 1):
        inside = jnp.where(x < side - d, pltpu.roll(cov, LANES - d, 1), 0.0)
        inside = inside + jnp.where(x >= d, pltpu.roll(cov, d, 1), 0.0)
        total = total + (SEAM + 1.0 - d) * inside

    @pl.when(jnp.logical_not(has_left))
    def _():
        left_ref[...] = jnp.zeros_like(left_ref)

    @pl.when(jnp.logical_not(has_right))
    def _():
        right_ref[...] = jnp.zeros_like(right_ref)

    @pl.when(has_right)
    def _():
        to_right().wait_send()
        to_left().wait_recv()

    @pl.when(has_left)
    def _():
        to_left().wait_send()
        to_right().wait_recv()

    left, right = left_ref[...], right_ref[...]
    for d in range(1, SEAM + 1):
        outside = jnp.where(x >= side - d, pltpu.roll(right, side - d, 1), 0.0)
        outside = outside + jnp.where(x < d, pltpu.roll(left, side + d, 1), 0.0)
        total = total + (SEAM + 1.0 - d) * outside
    total = total * (1.0 / (SEAM + 1) ** 2)
    out_ref[pl.ds(0, side // 2, stride=2), :] = total[:, :side]
    out_ref[pl.ds(1, side // 2, stride=2), :] = total[:, side:]


def tile_call(counts, emb, points, gauss, prompt, mask, sa_qkv, sa_out, t2i, t2i_out, up, down, i2t, i2t_out, hyper, gains):
    cells, width = emb.shape
    slots = points.shape[1]
    rows = 2 * slots * HEADS
    half = width // 2
    heads = slots * HEADS
    products = HEADS * (HEADS + 1) // 2 + 2 * HEADS + 2
    vmem = pl.BlockSpec(memory_space=pltpu.VMEM)
    return pl.pallas_call(
        tile_kernel,
        out_shape=(
            jax.ShapeDtypeStruct((slots, cells), BF16),
            jax.ShapeDtypeStruct((cells // LANES, LANES), F32),
        ),
        in_specs=[pl.BlockSpec(memory_space=pltpu.SMEM)] + [vmem] * 15,
        out_specs=(vmem, vmem),
        scratch_shapes=[
            pltpu.VMEM((cells, width), BF16),
            pltpu.VMEM((cells, width), BF16),
            pltpu.VMEM((2, math.isqrt(cells), half), F32),
            pltpu.VMEM((rows, cells), F32),
            pltpu.VMEM((rows, width), BF16),
            pltpu.VMEM((rows, LANES), F32),
            pltpu.VMEM((rows, LANES), F32),
            pltpu.VMEM((rows, width), F32),
            pltpu.VMEM((heads, width), BF16),
            pltpu.VMEM((heads + 2 * slots + GROUP, width), BF16),
            pltpu.VMEM((products, slots, LANES), F32),
            pltpu.VMEM((heads, CHUNK), F32),
            pltpu.VMEM((heads + 2 * slots + GROUP, CHUNK), F32),
        ],
        compiler_params=pltpu.CompilerParams(vmem_limit_bytes=56 * 2**20),
        name="tile",
    )(counts, emb, points, gauss, prompt, mask, sa_qkv, sa_out, t2i, t2i_out, up, down, i2t, i2t_out, hyper, gains)


def seam_call(cov, side, n):
    vmem = pl.BlockSpec(memory_space=pltpu.VMEM)
    return pl.pallas_call(
        functools.partial(seam_kernel, n),
        out_shape=jax.ShapeDtypeStruct((side, side), F32),
        in_specs=[vmem],
        out_specs=vmem,
        scratch_shapes=[
            pltpu.VMEM(cov.shape, F32),
            pltpu.VMEM(cov.shape, F32),
            pltpu.SemaphoreType.DMA((2,)),
            pltpu.SemaphoreType.DMA((2,)),
        ],
        compiler_params=pltpu.CompilerParams(collective_id=0, has_side_effects=True),
        name="seam",
    )(cov)


def shards(
    embedding,
    counts,
    points,
    pe_gauss,
    point_embed,
    mask_token,
    sa_qkv,
    sa_out,
    t2i_qkv,
    t2i_out,
    mlp_up,
    mlp_down,
    i2t_qkv,
    i2t_out,
    hyper_w,
    ln_gains,
):
    side, _, width = embedding.shape
    logits, cov = tile_call(
        counts,
        embedding.reshape(side * side, width),
        points[0, 0],
        pe_gauss,
        point_embed.reshape(1, width),
        mask_token.reshape(1, width),
        sa_qkv,
        sa_out,
        t2i_qkv,
        t2i_out,
        mlp_up,
        mlp_down,
        i2t_qkv,
        i2t_out,
        hyper_w,
        ln_gains,
    )
    blended = seam_call(cov, side, lax.axis_size("col"))
    return logits.reshape(1, 1, *logits.shape), blended


def solution(mesh):
    whole = [P()] * 13
    return jax.shard_map(
        shards,
        mesh=mesh,
        in_specs=(P("row", "col", None), P("col", None), P("row", "col", None, None), *whole),
        out_specs=(P("row", "col", None, None), P("row", "col")),
        check_vma=False,
    )
```

```python
import functools
import math

import jax
import jax.numpy as jnp
import numpy as np
from jax import lax
from jax.experimental import pallas as pl
from jax.experimental.pallas import tpu as pltpu
from jax.sharding import PartitionSpec as P

HEADS = 8
SEAM = 4
IMG = 1024
EPS = 1e-05
F32 = jnp.float32
BF16 = jnp.bfloat16
LANES = 128
GROUPS = 2
EMB_COPIES = 4
SCORE_CELLS = 1024
LARGE_SUM = 2.0**100
IMAGE_CELLS = 512


def turn_polynomials():
    z = np.linspace(0.0, 0.25, 4001)[1:]
    r = np.sqrt(z)
    fit = np.polynomial.chebyshev.Chebyshev.fit
    power = lambda c: [float(v) for v in c.convert(kind=np.polynomial.Polynomial, domain=[-1, 1]).coef]
    return (
        power(fit(z, np.sin(2 * math.pi * r) / r, 8, domain=[0.0, 0.25])),
        power(fit(z, np.cos(2 * math.pi * r), 8, domain=[0.0, 0.25])),
    )


SIN_COEF, COS_COEF = turn_polynomials()


def sin_cos_turns(turns):
    r = turns - jnp.floor(turns + 0.5)
    z = r * r
    s = jnp.full_like(z, SIN_COEF[-1])
    c = jnp.full_like(z, COS_COEF[-1])
    for a, b in zip(SIN_COEF[-2::-1], COS_COEF[-2::-1]):
        s = s * z + a
        c = c * z + b
    return s * r, c


def dot(a, b):
    return lax.dot_general(a, b, (((1,), (0,)), ((), ())), preferred_element_type=F32)


def dot_t(a, b):
    return lax.dot_general(a, b, (((1,), (1,)), ((), ())), preferred_element_type=F32)


def halves(values):
    high = values.astype(BF16)
    return high, (values - high.astype(F32)).astype(BF16)


def weight_dot(values, weight):
    rows = values.shape[0]
    both = dot(jnp.concatenate(halves(values), axis=0), weight)
    return both[:rows] + both[rows:]


def layer_norm(values, gain):
    centred = values - jnp.mean(values, axis=-1, keepdims=True)
    var = jnp.mean(centred * centred, axis=-1, keepdims=True)
    return centred * lax.rsqrt(var + EPS) * gain


def rounded(values):
    return values.astype(BF16).astype(F32)


def by_head(values):
    lane = lax.broadcasted_iota(jnp.int32, values.shape, 1) // (values.shape[1] // HEADS)
    return jnp.concatenate([jnp.where(lane == h, values, 0.0) for h in range(HEADS)], axis=0)


def centred_rows(values):
    return values - jnp.mean(values, axis=-1, keepdims=True)


def as_column(row):
    n = row.shape[1]
    i = lax.broadcasted_iota(jnp.int32, (n, n), 0)
    j = lax.broadcasted_iota(jnp.int32, (n, n), 1)
    return jnp.sum(jnp.where(i == j, jnp.broadcast_to(row, (n, n)), 0.0), axis=1, keepdims=True)


def tile_kernel(
    counts_ref,
    points_ref,
    gauss_ref,
    prompt_ref,
    mask_ref,
    gains_ref,
    emb_hbm,
    sa_qkv_hbm,
    sa_out_hbm,
    t2i_hbm,
    t2i_out_hbm,
    up_hbm,
    down_hbm,
    i2t_hbm,
    i2t_out_hbm,
    hyper_hbm,
    logits_hbm,
    cov_ref,
    emb_ref,
    sa_qkv_ref,
    sa_out_ref,
    t2i_ref,
    t2i_out_ref,
    up_ref,
    down_ref,
    i2t_ref,
    i2t_out_ref,
    hyper_ref,
    logits_ref,
    keys_ref,
    sq_ref,
    prob_ref,
    aq_ref,
    top_ref,
    sum_ref,
    start_ref,
    queries_ref,
    cross_ref,
    back_ref,
    hyper_out,
    gap_ref,
    row_ref,
    mix_ref,
    t_ref,
    table_ref,
    in_sem,
    emb_sem,
    out_sem,
):
    cells, width = emb_ref.shape
    slots = points_ref.shape[1]
    tokens = 2 * slots
    half = width // 2
    inner = t2i_ref.shape[1] // 3
    side = math.isqrt(cells)
    count = counts_ref[0, lax.axis_index("row")]

    weights = [
        pltpu.make_async_copy(source, target, in_sem.at[i])
        for i, (source, target) in enumerate(
            [
                (sa_qkv_hbm, sa_qkv_ref),
                (sa_out_hbm, sa_out_ref),
                (t2i_hbm, t2i_ref),
                (t2i_out_hbm, t2i_out_ref),
                (up_hbm, up_ref),
                (down_hbm, down_ref),
                (i2t_hbm, i2t_ref),
                (hyper_hbm, hyper_ref),
                (i2t_out_hbm, i2t_out_ref),
            ]
        )
    ]
    step = cells // EMB_COPIES
    cell_copies = [
        pltpu.make_async_copy(emb_hbm.at[pl.ds(i * step, step)], emb_ref.at[pl.ds(i * step, step)], emb_sem.at[i])
        for i in range(EMB_COPIES)
    ]
    for copy in weights[:3] + cell_copies + weights[3:]:
        copy.start()

    steps = (2.0 * (lax.broadcasted_iota(jnp.int32, (side, half), 0).astype(F32) + 0.5)) / side - 1.0
    sin_x, cos_x = sin_cos_turns(steps * gauss_ref[0:1, :])
    sin_y, cos_y = sin_cos_turns(steps * gauss_ref[1:2, :])

    coords = (2.0 * (points_ref[...].astype(F32) + 0.5)) / IMG - 1.0
    turns = as_column(coords[0:1, :]) * gauss_ref[0:1, :] + as_column(coords[1:2, :]) * gauss_ref[1:2, :]
    sin_p, cos_p = sin_cos_turns(turns)
    prompt = jnp.concatenate([sin_p, cos_p], axis=1) + prompt_ref[...]
    start = jnp.concatenate([jnp.broadcast_to(mask_ref[...], (slots, width)), prompt], axis=0)
    weights[0].wait()
    qkv = weight_dot(start, sa_qkv_ref[...])
    q, k, v = qkv[:, :width], qkv[:, width : 2 * width], qkv[:, 2 * width :]
    k_gap = k[slots:] - k[:slots]
    v_gap = v[slots:] - v[:slots]
    self_width = width // HEADS
    i = lax.broadcasted_iota(jnp.int32, (width, width), 0) // self_width
    j = lax.broadcasted_iota(jnp.int32, (width, width), 1) // self_width
    same = jnp.where(i == j, 1.0, 0.0).astype(BF16)
    gap = weight_dot(q * jnp.concatenate([k_gap, k_gap], axis=0), same) / math.sqrt(self_width)
    second = jax.nn.sigmoid(gap)
    joined = jnp.concatenate([v[:slots], v[:slots]], axis=0) + second * jnp.concatenate([v_gap, v_gap], axis=0)
    weights[1].wait()
    queries = layer_norm(weight_dot(joined, sa_out_ref[...]), gains_ref[0:1, :])
    weights[2].wait()
    cross_q = rounded(weight_dot(queries + start, t2i_ref[:, :inner]))
    scale = math.log2(math.e) / math.sqrt(inner // HEADS)
    aq_ref[...] = (dot_t(by_head(cross_q).astype(BF16), t2i_ref[:, inner : 2 * inner]) * scale).astype(BF16)

    table_ref[0] = sin_y
    table_ref[1] = cos_y
    start_ref[...] = start
    queries_ref[...] = queries

    for y in range(side):
        if y * side % step == 0:
            cell_copies[y * side // step].wait()
        rows = slice(y * side, (y + 1) * side)
        e = emb_ref[rows, :].astype(F32)
        sy, cy = table_ref[0, y : y + 1, :], table_ref[1, y : y + 1, :]
        e1, e2 = e[:, :half], e[:, half:]
        keys_ref[rows, :half] = (e1 + (sin_x * cy + cos_x * sy)).astype(BF16)
        keys_ref[rows, half:] = (e2 + (cos_x * cy - sin_x * sy)).astype(BF16)
        high, low = halves(e1 * e1 + e2 * e2)
        sq_ref[rows, :half] = high
        sq_ref[rows, half:] = low

    pairs = HEADS * tokens

    def scores(at):
        return dot_t(aq_ref[...], keys_ref[pl.ds(at, SCORE_CELLS), :])

    def probabilities(at, s):
        for r0 in range(0, pairs, 16):
            rows = slice(r0, r0 + 16)
            top = top_ref[rows, :]
            total = sum_ref[rows, :]
            for k0 in range(0, SCORE_CELLS, LANES):
                p = jnp.exp2(s[rows, k0 : k0 + LANES] - top)
                total = total + p
                prob_ref[rows, pl.ds(pl.multiple_of(at + k0, LANES), LANES)] = p.astype(BF16)
            sum_ref[rows, :] = total

    def prob_step(c, carry):
        at = pl.multiple_of(c * SCORE_CELLS, SCORE_CELLS)
        probabilities(at, scores(at))
        return carry

    sum_ref[...] = jnp.zeros_like(sum_ref)
    first = scores(0)
    top_ref[...] = jnp.broadcast_to(jnp.max(first, axis=1, keepdims=True), top_ref.shape)
    probabilities(0, first)
    lax.fori_loop(1, cells // SCORE_CELLS, prob_step, 0)

    @pl.when(jnp.logical_not(jnp.max(sum_ref[...]) < LARGE_SUM))
    def _():
        top_ref[...] = jnp.full(top_ref.shape, -jnp.inf, F32)

        def top_step(c, carry):
            s = scores(pl.multiple_of(c * SCORE_CELLS, SCORE_CELLS))
            for k0 in range(0, SCORE_CELLS, LANES):
                top_ref[...] = jnp.maximum(top_ref[...], s[:, k0 : k0 + LANES])
            return carry

        lax.fori_loop(0, cells // SCORE_CELLS, top_step, 0)
        top_ref[...] = jnp.broadcast_to(jnp.max(top_ref[...], axis=1, keepdims=True), top_ref.shape)
        sum_ref[...] = jnp.zeros_like(sum_ref)
        lax.fori_loop(0, cells // SCORE_CELLS, prob_step, 0)

    @pl.when(count > 0)
    def _():
        mean_cell = dot(prob_ref[...], emb_ref[...]) / jnp.sum(sum_ref[...], axis=1, keepdims=True)
        head_out = dot(mean_cell.astype(BF16), t2i_ref[:, 2 * inner :])
        lane = lax.broadcasted_iota(jnp.int32, (tokens, inner), 1) // (inner // HEADS)
        cross_out = jnp.zeros((tokens, inner), F32)
        for h in range(HEADS):
            cross_out = jnp.where(lane == h, head_out[h * tokens : (h + 1) * tokens], cross_out)
        cross_ref[...] = cross_out

    @pl.when(count > 0)
    def _():
        for copy in weights[3:]:
            copy.wait()
        queries = layer_norm(queries_ref[...] + weight_dot(cross_ref[...], t2i_out_ref[...]), gains_ref[1:2, :])
        hidden = jnp.maximum(weight_dot(queries, up_ref[...]), 0.0)
        queries = layer_norm(queries + weight_dot(hidden, down_ref[...]), gains_ref[2:3, :])
        start = start_ref[...]
        back_k = rounded(weight_dot(queries + start, i2t_ref[:, inner : 2 * inner]))
        back_v = rounded(weight_dot(queries, i2t_ref[:, 2 * inner :]))
        hyper = rounded(weight_dot(jnp.maximum(weight_dot(queries[:slots], hyper_ref[0]), 0.0), hyper_ref[1]))
        back_ref[0] = back_k
        back_ref[1] = back_v
        hyper_out[...] = hyper

    group = slots // GROUPS
    heads = HEADS * group
    lines = heads + 2 * group
    blank = width - heads

    @pl.when(count > 0)
    def _():
        back_k, back_v, hyper = back_ref[0], back_ref[1], hyper_out[...]
        key_gap = back_k[:slots] - back_k[slots:]
        gap_scale = 0.5 / math.sqrt(inner // HEADS)
        spread = 0.5 * (back_v[:slots] - back_v[slots:])
        middle = 0.5 * (back_v[:slots] + back_v[slots:])
        b_all = rounded(centred_rows(weight_dot(middle, i2t_out_ref[...])))
        g_all = rounded(centred_rows(hyper * gains_ref[3:4, :]))
        zeros = jnp.zeros((blank, width), BF16)
        r = lax.broadcasted_iota(jnp.int32, (lines, width), 0)
        c = lax.broadcasted_iota(jnp.int32, (lines, width), 1)
        own_slot = jnp.logical_and(r % group == c % group, c < heads)
        for n in range(GROUPS):
            of = slice(n * group, (n + 1) * group)
            gap_ref[n * heads : (n + 1) * heads, :] = (
                dot_t(by_head(key_gap[of]).astype(BF16), i2t_ref[:, :inner]) * gap_scale
            ).astype(BF16)
            u = rounded(centred_rows(dot(by_head(spread[of]).astype(BF16), i2t_out_ref[...])))
            b, g = b_all[of], g_all[of]
            left = jnp.concatenate([u, 2.0 * b, g], axis=0).astype(BF16)
            right = jnp.concatenate([u.astype(BF16), zeros], axis=0)
            constant = jnp.concatenate(
                [
                    jnp.zeros((heads, 1), F32),
                    jnp.sum(b * b, axis=1, keepdims=True),
                    jnp.sum(b * g, axis=1, keepdims=True),
                ],
                axis=0,
            )
            high = rounded(constant)
            mix = jnp.where(own_slot, dot_t(left, right), 0.0)
            mix = jnp.where(c == heads, high, jnp.where(c == heads + 1, constant - high, mix))
            mix_ref[n] = mix.astype(BF16)
            row_ref[n * lines : (n + 1) * lines, :] = jnp.concatenate([2.0 * u, 2.0 * b, g], axis=0).astype(BF16)

    ones = jnp.ones((16, width), BF16)
    row_ref[GROUPS * lines :, :] = ones
    t_ref[:, heads:, :] = jnp.ones((GROUPS, blank, cells), BF16)

    out_copies = []
    for at in range(0, cells, IMAGE_CELLS):
        here = slice(at, at + IMAGE_CELLS)
        t = jnp.tanh(dot_t(gap_ref[...], keys_ref[here, :])).astype(BF16)
        for n in range(GROUPS):
            t_ref[n, :heads, here] = t[n * heads : (n + 1) * heads]
        cell_part = dot_t(row_ref[...], emb_ref[here, :])
        sums = cell_part[GROUPS * lines : GROUPS * lines + 8]
        own = dot_t(ones, sq_ref[here, :])[:8] - sums * sums * (1.0 / width)
        logits = []
        for n in range(GROUPS):
            line = cell_part[n * lines : (n + 1) * lines] + dot(mix_ref[n], t_ref[n, :, here])
            t32 = t[n * heads : (n + 1) * heads].astype(F32)
            var = line[heads : heads + group] + jnp.concatenate([own] * (group // 8), axis=0)
            for h in range(HEADS):
                var = var + t32[h * group : (h + 1) * group] * line[h * group : (h + 1) * group]
            var = jnp.maximum(var, 0.0)
            logits.append(line[heads + group :] * lax.rsqrt(var + EPS * width))
        logit = rounded(jnp.concatenate(logits, axis=0))
        live = lax.broadcasted_iota(jnp.int32, logit.shape, 0) < count
        masked = jnp.where(live, logit, 0.0)
        logits_ref[:, here] = masked.astype(BF16)
        out_copies.append(pltpu.make_async_copy(logits_ref.at[:, here], logits_hbm.at[:, here], out_sem.at[at // IMAGE_CELLS]))
        out_copies[-1].start()
        cover = jnp.sum(jnp.where(live, jax.nn.sigmoid(masked), 0.0), axis=0, keepdims=True)
        for k0 in range(0, IMAGE_CELLS, LANES):
            cov_ref[(at + k0) // LANES : (at + k0) // LANES + 1, :] = cover[:, k0 : k0 + LANES]
    for copy in out_copies:
        copy.wait()


def seam_kernel(n, cov_ref, out_ref, left_ref, right_ref, send_sem, recv_sem):
    me = lax.axis_index("col")
    side = out_ref.shape[0]
    has_left, has_right = me > 0, me < n - 1
    barrier = pltpu.get_barrier_semaphore()
    mesh_id = pl.DeviceIdType.MESH

    def to_left():
        return pltpu.make_async_remote_copy(
            src_ref=cov_ref,
            dst_ref=right_ref,
            send_sem=send_sem.at[0],
            recv_sem=recv_sem.at[0],
            device_id={"col": me - 1},
            device_id_type=mesh_id,
        )

    def to_right():
        return pltpu.make_async_remote_copy(
            src_ref=cov_ref,
            dst_ref=left_ref,
            send_sem=send_sem.at[1],
            recv_sem=recv_sem.at[1],
            device_id={"col": me + 1},
            device_id_type=mesh_id,
        )

    @pl.when(has_left)
    def _():
        pl.semaphore_signal(barrier, inc=1, device_id={"col": me - 1}, device_id_type=mesh_id)

    @pl.when(has_right)
    def _():
        pl.semaphore_signal(barrier, inc=1, device_id={"col": me + 1}, device_id_type=mesh_id)

    pl.semaphore_wait(barrier, has_left.astype(jnp.int32) + has_right.astype(jnp.int32))

    @pl.when(has_left)
    def _():
        to_left().start()

    @pl.when(has_right)
    def _():
        to_right().start()

    cov = cov_ref[...]
    x = lax.broadcasted_iota(jnp.int32, cov.shape, 1) % side
    total = (SEAM + 1.0) * cov
    for d in range(1, SEAM + 1):
        inside = jnp.where(x < side - d, pltpu.roll(cov, LANES - d, 1), 0.0)
        inside = inside + jnp.where(x >= d, pltpu.roll(cov, d, 1), 0.0)
        total = total + (SEAM + 1.0 - d) * inside

    @pl.when(jnp.logical_not(has_left))
    def _():
        left_ref[...] = jnp.zeros_like(left_ref)

    @pl.when(jnp.logical_not(has_right))
    def _():
        right_ref[...] = jnp.zeros_like(right_ref)

    @pl.when(has_right)
    def _():
        to_right().wait_send()
        to_left().wait_recv()

    @pl.when(has_left)
    def _():
        to_left().wait_send()
        to_right().wait_recv()

    left, right = left_ref[...], right_ref[...]
    for d in range(1, SEAM + 1):
        outside = jnp.where(x >= side - d, pltpu.roll(right, side - d, 1), 0.0)
        outside = outside + jnp.where(x < d, pltpu.roll(left, side + d, 1), 0.0)
        total = total + (SEAM + 1.0 - d) * outside
    total = total * (1.0 / (SEAM + 1) ** 2)
    out_ref[pl.ds(0, side // 2, stride=2), :] = total[:, :side]
    out_ref[pl.ds(1, side // 2, stride=2), :] = total[:, side:]


def tile_call(counts, emb, points, gauss, prompt, mask, sa_qkv, sa_out, t2i, t2i_out, up, down, i2t, i2t_out, hyper, gains):
    cells, width = emb.shape
    slots = points.shape[1]
    rows = 2 * slots * HEADS
    heads = HEADS * slots // GROUPS
    lines = heads + 2 * slots // GROUPS
    vmem = pl.BlockSpec(memory_space=pltpu.VMEM)
    hbm = pl.BlockSpec(memory_space=pl.ANY)
    large = [emb, sa_qkv, sa_out, t2i, t2i_out, up, down, i2t, i2t_out, hyper]
    return pl.pallas_call(
        tile_kernel,
        out_shape=(
            jax.ShapeDtypeStruct((slots, cells), BF16),
            jax.ShapeDtypeStruct((cells // LANES, LANES), F32),
        ),
        in_specs=[pl.BlockSpec(memory_space=pltpu.SMEM)] + [vmem] * 5 + [hbm] * len(large),
        out_specs=(hbm, vmem),
        scratch_shapes=[pltpu.VMEM(a.shape, a.dtype) for a in large]
        + [
            pltpu.VMEM((slots, cells), BF16),
            pltpu.VMEM((cells, width), BF16),
            pltpu.VMEM((cells, width), BF16),
            pltpu.VMEM((rows, cells), BF16),
            pltpu.VMEM((rows, width), BF16),
            pltpu.VMEM((rows, LANES), F32),
            pltpu.VMEM((rows, LANES), F32),
            pltpu.VMEM((2 * slots, width), F32),
            pltpu.VMEM((2 * slots, width), F32),
            pltpu.VMEM((2 * slots, t2i.shape[1] // 3), F32),
            pltpu.VMEM((2, 2 * slots, t2i.shape[1] // 3), F32),
            pltpu.VMEM((slots, width), F32),
            pltpu.VMEM((GROUPS * heads, width), BF16),
            pltpu.VMEM((GROUPS * lines + 16, width), BF16),
            pltpu.VMEM((GROUPS, lines, width), BF16),
            pltpu.VMEM((GROUPS, width, cells), BF16),
            pltpu.VMEM((2, math.isqrt(cells), width // 2), F32),
            pltpu.SemaphoreType.DMA((len(large) - 1,)),
            pltpu.SemaphoreType.DMA((EMB_COPIES,)),
            pltpu.SemaphoreType.DMA((cells // IMAGE_CELLS,)),
        ],
        compiler_params=pltpu.CompilerParams(vmem_limit_bytes=58 * 2**20),
        name="tile",
    )(counts, points, gauss, prompt, mask, gains, *large)


def seam_call(cov, side, n):
    vmem = pl.BlockSpec(memory_space=pltpu.VMEM)
    return pl.pallas_call(
        functools.partial(seam_kernel, n),
        out_shape=jax.ShapeDtypeStruct((side, side), F32),
        in_specs=[vmem],
        out_specs=vmem,
        scratch_shapes=[
            pltpu.VMEM(cov.shape, F32),
            pltpu.VMEM(cov.shape, F32),
            pltpu.SemaphoreType.DMA((2,)),
            pltpu.SemaphoreType.DMA((2,)),
        ],
        compiler_params=pltpu.CompilerParams(collective_id=0, has_side_effects=True),
        name="seam",
    )(cov)


def shards(
    embedding,
    counts,
    points,
    pe_gauss,
    point_embed,
    mask_token,
    sa_qkv,
    sa_out,
    t2i_qkv,
    t2i_out,
    mlp_up,
    mlp_down,
    i2t_qkv,
    i2t_out,
    hyper_w,
    ln_gains,
):
    side, _, width = embedding.shape
    logits, cov = tile_call(
        counts,
        embedding.reshape(side * side, width),
        points[0, 0],
        pe_gauss,
        point_embed.reshape(1, width),
        mask_token.reshape(1, width),
        sa_qkv,
        sa_out,
        t2i_qkv,
        t2i_out,
        mlp_up,
        mlp_down,
        i2t_qkv,
        i2t_out,
        hyper_w,
        ln_gains,
    )
    blended = seam_call(cov, side, lax.axis_size("col"))
    return logits.reshape(1, 1, *logits.shape), blended


def solution(mesh):
    whole = [P()] * 13
    return jax.shard_map(
        shards,
        mesh=mesh,
        in_specs=(P("row", "col", None), P("col", None), P("row", "col", None, None), *whole),
        out_specs=(P("row", "col", None, None), P("row", "col")),
        check_vma=False,
    )
```

```python
import functools
import math

import jax
import jax.numpy as jnp
import numpy as np
from jax import lax
from jax.experimental import pallas as pl
from jax.experimental.pallas import tpu as pltpu
from jax.sharding import PartitionSpec as P

HEADS = 8
SEAM = 4
IMG = 1024
EPS = 1e-05
F32 = jnp.float32
BF16 = jnp.bfloat16
LANES = 128
GROUPS = 2
EMB_COPIES = 4
SCORE_CELLS = 1024
LARGE_SUM = 2.0**100
IMAGE_CELLS = 512


def turn_polynomials():
    z = np.linspace(0.0, 0.25, 4001)[1:]
    r = np.sqrt(z)
    fit = np.polynomial.chebyshev.Chebyshev.fit
    power = lambda c: [float(v) for v in c.convert(kind=np.polynomial.Polynomial, domain=[-1, 1]).coef]
    return (
        power(fit(z, np.sin(2 * math.pi * r) / r, 8, domain=[0.0, 0.25])),
        power(fit(z, np.cos(2 * math.pi * r), 8, domain=[0.0, 0.25])),
    )


SIN_COEF, COS_COEF = turn_polynomials()


def sin_cos_turns(turns):
    r = turns - jnp.floor(turns + 0.5)
    z = r * r
    s = jnp.full_like(z, SIN_COEF[-1])
    c = jnp.full_like(z, COS_COEF[-1])
    for a, b in zip(SIN_COEF[-2::-1], COS_COEF[-2::-1]):
        s = s * z + a
        c = c * z + b
    return s * r, c


def dot(a, b):
    return lax.dot_general(a, b, (((1,), (0,)), ((), ())), preferred_element_type=F32)


def dot_t(a, b):
    return lax.dot_general(a, b, (((1,), (1,)), ((), ())), preferred_element_type=F32)


def halves(values):
    high = values.astype(BF16)
    return high, (values - high.astype(F32)).astype(BF16)


def weight_dot(values, weight):
    rows = values.shape[0]
    both = dot(jnp.concatenate(halves(values), axis=0), weight)
    return both[:rows] + both[rows:]


def layer_norm(values, gain):
    centred = values - jnp.mean(values, axis=-1, keepdims=True)
    var = jnp.mean(centred * centred, axis=-1, keepdims=True)
    return centred * lax.rsqrt(var + EPS) * gain


def rounded(values):
    return values.astype(BF16).astype(F32)


def by_head(values):
    lane = lax.broadcasted_iota(jnp.int32, values.shape, 1) // (values.shape[1] // HEADS)
    return jnp.concatenate([jnp.where(lane == h, values, 0.0) for h in range(HEADS)], axis=0)


def centred_rows(values):
    return values - jnp.mean(values, axis=-1, keepdims=True)


def as_column(row):
    n = row.shape[1]
    i = lax.broadcasted_iota(jnp.int32, (n, n), 0)
    j = lax.broadcasted_iota(jnp.int32, (n, n), 1)
    return jnp.sum(jnp.where(i == j, jnp.broadcast_to(row, (n, n)), 0.0), axis=1, keepdims=True)


def tile_kernel(
    counts_ref,
    points_ref,
    gauss_ref,
    prompt_ref,
    mask_ref,
    gains_ref,
    emb_hbm,
    sa_qkv_hbm,
    sa_out_hbm,
    t2i_hbm,
    t2i_out_hbm,
    up_hbm,
    down_hbm,
    i2t_hbm,
    i2t_out_hbm,
    hyper_hbm,
    logits_hbm,
    cov_ref,
    emb_ref,
    sa_qkv_ref,
    sa_out_ref,
    t2i_ref,
    t2i_out_ref,
    up_ref,
    down_ref,
    i2t_ref,
    i2t_out_ref,
    hyper_ref,
    logits_ref,
    keys_ref,
    prob_ref,
    aq_ref,
    top_ref,
    sum_ref,
    start_ref,
    queries_ref,
    cross_ref,
    back_ref,
    hyper_out,
    gap_ref,
    row_ref,
    mix_ref,
    t_ref,
    table_ref,
    in_sem,
    emb_sem,
    out_sem,
):
    cells, width = emb_ref.shape
    slots = points_ref.shape[1]
    tokens = 2 * slots
    half = width // 2
    inner = t2i_ref.shape[1] // 3
    side = math.isqrt(cells)
    count = counts_ref[0, lax.axis_index("row")]

    weights = [
        pltpu.make_async_copy(source, target, in_sem.at[i])
        for i, (source, target) in enumerate(
            [
                (sa_qkv_hbm, sa_qkv_ref),
                (sa_out_hbm, sa_out_ref),
                (t2i_hbm, t2i_ref),
                (t2i_out_hbm, t2i_out_ref),
                (up_hbm, up_ref),
                (down_hbm, down_ref),
                (i2t_hbm, i2t_ref),
                (hyper_hbm, hyper_ref),
                (i2t_out_hbm, i2t_out_ref),
            ]
        )
    ]
    step = cells // EMB_COPIES
    cell_copies = [
        pltpu.make_async_copy(emb_hbm.at[pl.ds(i * step, step)], emb_ref.at[pl.ds(i * step, step)], emb_sem.at[i])
        for i in range(EMB_COPIES)
    ]
    for copy in weights[:3] + cell_copies + weights[3:]:
        copy.start()

    steps = (2.0 * (lax.broadcasted_iota(jnp.int32, (side, half), 0).astype(F32) + 0.5)) / side - 1.0
    sin_x, cos_x = sin_cos_turns(steps * gauss_ref[0:1, :])
    sin_y, cos_y = sin_cos_turns(steps * gauss_ref[1:2, :])

    coords = (2.0 * (points_ref[...].astype(F32) + 0.5)) / IMG - 1.0
    turns = as_column(coords[0:1, :]) * gauss_ref[0:1, :] + as_column(coords[1:2, :]) * gauss_ref[1:2, :]
    sin_p, cos_p = sin_cos_turns(turns)
    prompt = jnp.concatenate([sin_p, cos_p], axis=1) + prompt_ref[...]
    start = jnp.concatenate([jnp.broadcast_to(mask_ref[...], (slots, width)), prompt], axis=0)
    weights[0].wait()
    qkv = weight_dot(start, sa_qkv_ref[...])
    q, k, v = qkv[:, :width], qkv[:, width : 2 * width], qkv[:, 2 * width :]
    k_gap = k[slots:] - k[:slots]
    v_gap = v[slots:] - v[:slots]
    self_width = width // HEADS
    i = lax.broadcasted_iota(jnp.int32, (width, width), 0) // self_width
    j = lax.broadcasted_iota(jnp.int32, (width, width), 1) // self_width
    same = jnp.where(i == j, 1.0, 0.0).astype(BF16)
    gap = weight_dot(q * jnp.concatenate([k_gap, k_gap], axis=0), same) / math.sqrt(self_width)
    second = jax.nn.sigmoid(gap)
    joined = jnp.concatenate([v[:slots], v[:slots]], axis=0) + second * jnp.concatenate([v_gap, v_gap], axis=0)
    weights[1].wait()
    queries = layer_norm(weight_dot(joined, sa_out_ref[...]), gains_ref[0:1, :])
    weights[2].wait()
    cross_q = rounded(weight_dot(queries + start, t2i_ref[:, :inner]))
    scale = math.log2(math.e) / math.sqrt(inner // HEADS)
    aq_ref[...] = (dot_t(by_head(cross_q).astype(BF16), t2i_ref[:, inner : 2 * inner]) * scale).astype(BF16)

    table_ref[0] = sin_y
    table_ref[1] = cos_y
    start_ref[...] = start
    queries_ref[...] = queries

    for y in range(side):
        if y * side % step == 0:
            cell_copies[y * side // step].wait()
        rows = slice(y * side, (y + 1) * side)
        e = emb_ref[rows, :].astype(F32)
        sy, cy = table_ref[0, y : y + 1, :], table_ref[1, y : y + 1, :]
        e1, e2 = e[:, :half], e[:, half:]
        keys_ref[rows, :half] = (e1 + (sin_x * cy + cos_x * sy)).astype(BF16)
        keys_ref[rows, half:] = (e2 + (cos_x * cy - sin_x * sy)).astype(BF16)

    pairs = HEADS * tokens

    def scores(at):
        return dot_t(aq_ref[...], keys_ref[pl.ds(at, SCORE_CELLS), :])

    def probabilities(at, s):
        for r0 in range(0, pairs, 16):
            rows = slice(r0, r0 + 16)
            top = top_ref[rows, :]
            total = sum_ref[rows, :]
            for k0 in range(0, SCORE_CELLS, LANES):
                p = jnp.exp2(s[rows, k0 : k0 + LANES] - top)
                total = total + p
                prob_ref[rows, pl.ds(pl.multiple_of(at + k0, LANES), LANES)] = p.astype(BF16)
            sum_ref[rows, :] = total

    def prob_step(c, carry):
        at = pl.multiple_of(c * SCORE_CELLS, SCORE_CELLS)
        probabilities(at, scores(at))
        return carry

    sum_ref[...] = jnp.zeros_like(sum_ref)
    first = scores(0)
    top_ref[...] = jnp.broadcast_to(jnp.max(first, axis=1, keepdims=True), top_ref.shape)
    probabilities(0, first)
    lax.fori_loop(1, cells // SCORE_CELLS, prob_step, 0)

    @pl.when(jnp.logical_not(jnp.max(sum_ref[...]) < LARGE_SUM))
    def _():
        top_ref[...] = jnp.full(top_ref.shape, -jnp.inf, F32)

        def top_step(c, carry):
            s = scores(pl.multiple_of(c * SCORE_CELLS, SCORE_CELLS))
            for k0 in range(0, SCORE_CELLS, LANES):
                top_ref[...] = jnp.maximum(top_ref[...], s[:, k0 : k0 + LANES])
            return carry

        lax.fori_loop(0, cells // SCORE_CELLS, top_step, 0)
        top_ref[...] = jnp.broadcast_to(jnp.max(top_ref[...], axis=1, keepdims=True), top_ref.shape)
        sum_ref[...] = jnp.zeros_like(sum_ref)
        lax.fori_loop(0, cells // SCORE_CELLS, prob_step, 0)

    @pl.when(count > 0)
    def _():
        mean_cell = dot(prob_ref[...], emb_ref[...]) / jnp.sum(sum_ref[...], axis=1, keepdims=True)
        head_out = dot(mean_cell.astype(BF16), t2i_ref[:, 2 * inner :])
        lane = lax.broadcasted_iota(jnp.int32, (tokens, inner), 1) // (inner // HEADS)
        cross_out = jnp.zeros((tokens, inner), F32)
        for h in range(HEADS):
            cross_out = jnp.where(lane == h, head_out[h * tokens : (h + 1) * tokens], cross_out)
        cross_ref[...] = cross_out

    @pl.when(count > 0)
    def _():
        for copy in weights[3:]:
            copy.wait()
        queries = layer_norm(queries_ref[...] + weight_dot(cross_ref[...], t2i_out_ref[...]), gains_ref[1:2, :])
        hidden = jnp.maximum(dot(queries.astype(BF16), up_ref[...]), 0.0)
        queries = layer_norm(queries + dot(hidden.astype(BF16), down_ref[...]), gains_ref[2:3, :])
        start = start_ref[...]
        back_k = rounded(weight_dot(queries + start, i2t_ref[:, inner : 2 * inner]))
        back_v = rounded(weight_dot(queries, i2t_ref[:, 2 * inner :]))
        hyper = rounded(weight_dot(jnp.maximum(weight_dot(queries[:slots], hyper_ref[0]), 0.0), hyper_ref[1]))
        back_ref[0] = back_k
        back_ref[1] = back_v
        hyper_out[...] = hyper

    group = slots // GROUPS
    heads = HEADS * group
    lines = heads + 2 * group
    blank = width - heads

    @pl.when(count > 0)
    def _():
        back_k, back_v, hyper = back_ref[0], back_ref[1], hyper_out[...]
        key_gap = back_k[:slots] - back_k[slots:]
        gap_scale = 0.5 / math.sqrt(inner // HEADS)
        spread = 0.5 * (back_v[:slots] - back_v[slots:])
        middle = 0.5 * (back_v[:slots] + back_v[slots:])
        b_all = rounded(centred_rows(weight_dot(middle, i2t_out_ref[...])))
        g_all = rounded(centred_rows(hyper * gains_ref[3:4, :]))
        zeros = jnp.zeros((blank, width), BF16)
        r = lax.broadcasted_iota(jnp.int32, (lines, width), 0)
        c = lax.broadcasted_iota(jnp.int32, (lines, width), 1)
        own_slot = jnp.logical_and(r % group == c % group, c < heads)
        for n in range(GROUPS):
            of = slice(n * group, (n + 1) * group)
            gap_ref[n * heads : (n + 1) * heads, :] = (
                dot_t(by_head(key_gap[of]).astype(BF16), i2t_ref[:, :inner]) * gap_scale
            ).astype(BF16)
            u = rounded(centred_rows(dot(by_head(spread[of]).astype(BF16), i2t_out_ref[...])))
            b, g = b_all[of], g_all[of]
            left = jnp.concatenate([u, 2.0 * b, g], axis=0).astype(BF16)
            right = jnp.concatenate([u.astype(BF16), zeros], axis=0)
            constant = jnp.concatenate(
                [
                    jnp.zeros((heads, 1), F32),
                    jnp.sum(b * b, axis=1, keepdims=True),
                    jnp.sum(b * g, axis=1, keepdims=True),
                ],
                axis=0,
            )
            high = rounded(constant)
            mix = jnp.where(own_slot, dot_t(left, right), 0.0)
            mix = jnp.where(c == heads, high, jnp.where(c == heads + 1, constant - high, mix))
            mix_ref[n] = mix.astype(BF16)
            row_ref[n * lines : (n + 1) * lines, :] = jnp.concatenate([2.0 * u, 2.0 * b, g], axis=0).astype(BF16)

    ones = jnp.ones((16, width), BF16)
    row_ref[GROUPS * lines :, :] = ones
    t_ref[:, heads:, :] = jnp.ones((GROUPS, blank, cells), BF16)

    out_copies = []
    for at in range(0, cells, IMAGE_CELLS):
        here = slice(at, at + IMAGE_CELLS)
        t = jnp.tanh(dot_t(gap_ref[...], keys_ref[here, :])).astype(BF16)
        for n in range(GROUPS):
            t_ref[n, :heads, here] = t[n * heads : (n + 1) * heads]
        cell_part = dot_t(row_ref[...], emb_ref[here, :])
        sums = cell_part[GROUPS * lines : GROUPS * lines + 8]
        e = emb_ref[here, :].astype(F32)
        squares = jnp.concatenate(halves(e[:, :half] * e[:, :half] + e[:, half:] * e[:, half:]), axis=1)
        own = dot_t(ones, squares)[:8] - sums * sums * (1.0 / width)
        logits = []
        for n in range(GROUPS):
            line = cell_part[n * lines : (n + 1) * lines] + dot(mix_ref[n], t_ref[n, :, here])
            t32 = t[n * heads : (n + 1) * heads].astype(F32)
            var = line[heads : heads + group] + jnp.concatenate([own] * (group // 8), axis=0)
            for h in range(HEADS):
                var = var + t32[h * group : (h + 1) * group] * line[h * group : (h + 1) * group]
            var = jnp.maximum(var, 0.0)
            logits.append(line[heads + group :] * lax.rsqrt(var + EPS * width))
        logit = rounded(jnp.concatenate(logits, axis=0))
        live = lax.broadcasted_iota(jnp.int32, logit.shape, 0) < count
        masked = jnp.where(live, logit, 0.0)
        logits_ref[:, here] = masked.astype(BF16)
        out_copies.append(pltpu.make_async_copy(logits_ref.at[:, here], logits_hbm.at[:, here], out_sem.at[at // IMAGE_CELLS]))
        out_copies[-1].start()
        cover = jnp.sum(jnp.where(live, jax.nn.sigmoid(masked), 0.0), axis=0, keepdims=True)
        for k0 in range(0, IMAGE_CELLS, LANES):
            cov_ref[(at + k0) // LANES : (at + k0) // LANES + 1, :] = cover[:, k0 : k0 + LANES]
    for copy in out_copies:
        copy.wait()


def seam_kernel(n, cov_hbm, out_ref, cov_ref, left_ref, right_ref, send_sem, recv_sem, own_sem):
    me = lax.axis_index("col")
    side = out_ref.shape[0]
    has_left, has_right = me > 0, me < n - 1
    barrier = pltpu.get_barrier_semaphore()
    mesh_id = pl.DeviceIdType.MESH
    own_copy = pltpu.make_async_copy(cov_hbm, cov_ref, own_sem)
    own_copy.start()

    def to_left():
        return pltpu.make_async_remote_copy(
            src_ref=cov_hbm,
            dst_ref=right_ref,
            send_sem=send_sem.at[0],
            recv_sem=recv_sem.at[0],
            device_id={"col": me - 1},
            device_id_type=mesh_id,
        )

    def to_right():
        return pltpu.make_async_remote_copy(
            src_ref=cov_hbm,
            dst_ref=left_ref,
            send_sem=send_sem.at[1],
            recv_sem=recv_sem.at[1],
            device_id={"col": me + 1},
            device_id_type=mesh_id,
        )

    @pl.when(has_left)
    def _():
        pl.semaphore_signal(barrier, inc=1, device_id={"col": me - 1}, device_id_type=mesh_id)

    @pl.when(has_right)
    def _():
        pl.semaphore_signal(barrier, inc=1, device_id={"col": me + 1}, device_id_type=mesh_id)

    pl.semaphore_wait(barrier, has_left.astype(jnp.int32) + has_right.astype(jnp.int32))

    @pl.when(has_left)
    def _():
        to_left().start()

    @pl.when(has_right)
    def _():
        to_right().start()

    own_copy.wait()
    cov = cov_ref[...]
    x = lax.broadcasted_iota(jnp.int32, cov.shape, 1) % side
    total = (SEAM + 1.0) * cov
    for d in range(1, SEAM + 1):
        inside = jnp.where(x < side - d, pltpu.roll(cov, LANES - d, 1), 0.0)
        inside = inside + jnp.where(x >= d, pltpu.roll(cov, d, 1), 0.0)
        total = total + (SEAM + 1.0 - d) * inside

    @pl.when(jnp.logical_not(has_left))
    def _():
        left_ref[...] = jnp.zeros_like(left_ref)

    @pl.when(jnp.logical_not(has_right))
    def _():
        right_ref[...] = jnp.zeros_like(right_ref)

    @pl.when(has_right)
    def _():
        to_right().wait_send()
        to_left().wait_recv()

    @pl.when(has_left)
    def _():
        to_left().wait_send()
        to_right().wait_recv()

    left, right = left_ref[...], right_ref[...]
    for d in range(1, SEAM + 1):
        outside = jnp.where(x >= side - d, pltpu.roll(right, side - d, 1), 0.0)
        outside = outside + jnp.where(x < d, pltpu.roll(left, side + d, 1), 0.0)
        total = total + (SEAM + 1.0 - d) * outside
    total = total * (1.0 / (SEAM + 1) ** 2)
    out_ref[pl.ds(0, side // 2, stride=2), :] = total[:, :side]
    out_ref[pl.ds(1, side // 2, stride=2), :] = total[:, side:]


def tile_call(counts, emb, points, gauss, prompt, mask, sa_qkv, sa_out, t2i, t2i_out, up, down, i2t, i2t_out, hyper, gains):
    cells, width = emb.shape
    slots = points.shape[1]
    rows = 2 * slots * HEADS
    heads = HEADS * slots // GROUPS
    lines = heads + 2 * slots // GROUPS
    vmem = pl.BlockSpec(memory_space=pltpu.VMEM)
    hbm = pl.BlockSpec(memory_space=pl.ANY)
    large = [emb, sa_qkv, sa_out, t2i, t2i_out, up, down, i2t, i2t_out, hyper]
    return pl.pallas_call(
        tile_kernel,
        out_shape=(
            jax.ShapeDtypeStruct((slots, cells), BF16),
            jax.ShapeDtypeStruct((cells // LANES, LANES), F32),
        ),
        in_specs=[pl.BlockSpec(memory_space=pltpu.SMEM)] + [vmem] * 5 + [hbm] * len(large),
        out_specs=(hbm, vmem),
        scratch_shapes=[pltpu.VMEM(a.shape, a.dtype) for a in large]
        + [
            pltpu.VMEM((slots, cells), BF16),
            pltpu.VMEM((cells, width), BF16),
            pltpu.VMEM((rows, cells), BF16),
            pltpu.VMEM((rows, width), BF16),
            pltpu.VMEM((rows, LANES), F32),
            pltpu.VMEM((rows, LANES), F32),
            pltpu.VMEM((2 * slots, width), F32),
            pltpu.VMEM((2 * slots, width), F32),
            pltpu.VMEM((2 * slots, t2i.shape[1] // 3), F32),
            pltpu.VMEM((2, 2 * slots, t2i.shape[1] // 3), F32),
            pltpu.VMEM((slots, width), F32),
            pltpu.VMEM((GROUPS * heads, width), BF16),
            pltpu.VMEM((GROUPS * lines + 16, width), BF16),
            pltpu.VMEM((GROUPS, lines, width), BF16),
            pltpu.VMEM((GROUPS, width, cells), BF16),
            pltpu.VMEM((2, math.isqrt(cells), width // 2), F32),
            pltpu.SemaphoreType.DMA((len(large) - 1,)),
            pltpu.SemaphoreType.DMA((EMB_COPIES,)),
            pltpu.SemaphoreType.DMA((cells // IMAGE_CELLS,)),
        ],
        compiler_params=pltpu.CompilerParams(vmem_limit_bytes=58 * 2**20),
        name="tile",
    )(counts, points, gauss, prompt, mask, gains, *large)


def seam_call(cov, side, n):
    vmem = pl.BlockSpec(memory_space=pltpu.VMEM)
    return pl.pallas_call(
        functools.partial(seam_kernel, n),
        out_shape=jax.ShapeDtypeStruct((side, side), F32),
        in_specs=[pl.BlockSpec(memory_space=pl.ANY)],
        out_specs=vmem,
        scratch_shapes=[
            pltpu.VMEM(cov.shape, F32),
            pltpu.VMEM(cov.shape, F32),
            pltpu.VMEM(cov.shape, F32),
            pltpu.SemaphoreType.DMA((2,)),
            pltpu.SemaphoreType.DMA((2,)),
            pltpu.SemaphoreType.DMA(()),
        ],
        compiler_params=pltpu.CompilerParams(collective_id=0, has_side_effects=True),
        name="seam",
    )(cov)


def shards(
    embedding,
    counts,
    points,
    pe_gauss,
    point_embed,
    mask_token,
    sa_qkv,
    sa_out,
    t2i_qkv,
    t2i_out,
    mlp_up,
    mlp_down,
    i2t_qkv,
    i2t_out,
    hyper_w,
    ln_gains,
):
    side, _, width = embedding.shape
    logits, cov = tile_call(
        counts,
        embedding.reshape(side * side, width),
        points[0, 0],
        pe_gauss,
        point_embed.reshape(1, width),
        mask_token.reshape(1, width),
        sa_qkv,
        sa_out,
        t2i_qkv,
        t2i_out,
        mlp_up,
        mlp_down,
        i2t_qkv,
        i2t_out,
        hyper_w,
        ln_gains,
    )
    blended = seam_call(cov, side, lax.axis_size("col"))
    return logits.reshape(1, 1, *logits.shape), blended


def solution(mesh):
    whole = [P()] * 13
    return jax.shard_map(
        shards,
        mesh=mesh,
        in_specs=(P("row", "col", None), P("col", None), P("row", "col", None, None), *whole),
        out_specs=(P("row", "col", None, None), P("row", "col")),
        check_vma=False,
    )
```

```python
import functools
import math

import jax
import jax.numpy as jnp
import numpy as np
from jax import lax
from jax.experimental import pallas as pl
from jax.experimental.pallas import tpu as pltpu
from jax.sharding import PartitionSpec as P

HEADS = 8
SEAM = 4
IMG = 1024
EPS = 1e-05
F32 = jnp.float32
BF16 = jnp.bfloat16
LANES = 128
GROUPS = 2
EMB_COPIES = 4
SCORE_CELLS = 1024
LARGE_SUM = 2.0**100
IMAGE_CELLS = 512


def turn_polynomials():
    z = np.linspace(0.0, 0.25, 4001)[1:]
    r = np.sqrt(z)
    fit = np.polynomial.chebyshev.Chebyshev.fit
    power = lambda c: [float(v) for v in c.convert(kind=np.polynomial.Polynomial, domain=[-1, 1]).coef]
    return (
        power(fit(z, np.sin(2 * math.pi * r) / r, 8, domain=[0.0, 0.25])),
        power(fit(z, np.cos(2 * math.pi * r), 8, domain=[0.0, 0.25])),
    )


SIN_COEF, COS_COEF = turn_polynomials()


def sin_cos_turns(turns):
    r = turns - jnp.floor(turns + 0.5)
    z = r * r
    s = jnp.full_like(z, SIN_COEF[-1])
    c = jnp.full_like(z, COS_COEF[-1])
    for a, b in zip(SIN_COEF[-2::-1], COS_COEF[-2::-1]):
        s = s * z + a
        c = c * z + b
    return s * r, c


def dot(a, b):
    return lax.dot_general(a, b, (((1,), (0,)), ((), ())), preferred_element_type=F32)


def dot_t(a, b):
    return lax.dot_general(a, b, (((1,), (1,)), ((), ())), preferred_element_type=F32)


def halves(values):
    high = values.astype(BF16)
    return high, (values - high.astype(F32)).astype(BF16)


def weight_dot(values, weight):
    rows = values.shape[0]
    both = dot(jnp.concatenate(halves(values), axis=0), weight)
    return both[:rows] + both[rows:]


def layer_norm(values, gain):
    centred = values - jnp.mean(values, axis=-1, keepdims=True)
    var = jnp.mean(centred * centred, axis=-1, keepdims=True)
    return centred * lax.rsqrt(var + EPS) * gain


def rounded(values):
    return values.astype(BF16).astype(F32)


def by_head(values):
    lane = lax.broadcasted_iota(jnp.int32, values.shape, 1) // (values.shape[1] // HEADS)
    return jnp.concatenate([jnp.where(lane == h, values, 0.0) for h in range(HEADS)], axis=0)


def centred_rows(values):
    return values - jnp.mean(values, axis=-1, keepdims=True)


def as_column(row):
    n = row.shape[1]
    i = lax.broadcasted_iota(jnp.int32, (n, n), 0)
    j = lax.broadcasted_iota(jnp.int32, (n, n), 1)
    return jnp.sum(jnp.where(i == j, jnp.broadcast_to(row, (n, n)), 0.0), axis=1, keepdims=True)


def tile_kernel(
    counts_ref,
    points_ref,
    gauss_ref,
    prompt_ref,
    mask_ref,
    gains_ref,
    emb_hbm,
    sa_qkv_hbm,
    sa_out_hbm,
    t2i_hbm,
    t2i_out_hbm,
    up_hbm,
    down_hbm,
    i2t_hbm,
    i2t_out_hbm,
    hyper_hbm,
    logits_hbm,
    cov_ref,
    tail_ref,
    emb_ref,
    sa_qkv_ref,
    sa_out_ref,
    t2i_ref,
    t2i_out_ref,
    up_ref,
    down_ref,
    i2t_ref,
    i2t_out_ref,
    hyper_ref,
    logits_ref,
    keys_ref,
    prob_ref,
    aq_ref,
    top_ref,
    sum_ref,
    start_ref,
    queries_ref,
    cross_ref,
    back_ref,
    hyper_out,
    gap_ref,
    row_ref,
    mix_ref,
    t_ref,
    table_ref,
    in_sem,
    emb_sem,
    out_sem,
):
    cells, width = emb_ref.shape
    slots = points_ref.shape[1]
    tokens = 2 * slots
    half = width // 2
    inner = t2i_ref.shape[1] // 3
    side = math.isqrt(cells)
    count = counts_ref[0, lax.axis_index("row")]

    weights = [
        pltpu.make_async_copy(source, target, in_sem.at[i])
        for i, (source, target) in enumerate(
            [
                (sa_qkv_hbm, sa_qkv_ref),
                (sa_out_hbm, sa_out_ref),
                (t2i_hbm, t2i_ref),
                (t2i_out_hbm, t2i_out_ref),
                (up_hbm, up_ref),
                (down_hbm, down_ref),
                (i2t_hbm, i2t_ref),
                (hyper_hbm, hyper_ref),
                (i2t_out_hbm, i2t_out_ref),
            ]
        )
    ]
    step = cells // EMB_COPIES
    cell_copies = [
        pltpu.make_async_copy(emb_hbm.at[pl.ds(i * step, step)], emb_ref.at[pl.ds(i * step, step)], emb_sem.at[i])
        for i in range(EMB_COPIES)
    ]
    for copy in weights[:3] + cell_copies + weights[3:]:
        copy.start()

    steps = (2.0 * (lax.broadcasted_iota(jnp.int32, (side, half), 0).astype(F32) + 0.5)) / side - 1.0
    sin_x, cos_x = sin_cos_turns(steps * gauss_ref[0:1, :])
    sin_y, cos_y = sin_cos_turns(steps * gauss_ref[1:2, :])

    coords = (2.0 * (points_ref[...].astype(F32) + 0.5)) / IMG - 1.0
    turns = as_column(coords[0:1, :]) * gauss_ref[0:1, :] + as_column(coords[1:2, :]) * gauss_ref[1:2, :]
    sin_p, cos_p = sin_cos_turns(turns)
    prompt = jnp.concatenate([sin_p, cos_p], axis=1) + prompt_ref[...]
    start = jnp.concatenate([jnp.broadcast_to(mask_ref[...], (slots, width)), prompt], axis=0)
    weights[0].wait()
    qkv = weight_dot(start, sa_qkv_ref[...])
    q, k, v = qkv[:, :width], qkv[:, width : 2 * width], qkv[:, 2 * width :]
    k_gap = k[slots:] - k[:slots]
    v_gap = v[slots:] - v[:slots]
    self_width = width // HEADS
    i = lax.broadcasted_iota(jnp.int32, (width, width), 0) // self_width
    j = lax.broadcasted_iota(jnp.int32, (width, width), 1) // self_width
    same = jnp.where(i == j, 1.0, 0.0).astype(BF16)
    gap = weight_dot(q * jnp.concatenate([k_gap, k_gap], axis=0), same) / math.sqrt(self_width)
    second = jax.nn.sigmoid(gap)
    joined = jnp.concatenate([v[:slots], v[:slots]], axis=0) + second * jnp.concatenate([v_gap, v_gap], axis=0)
    weights[1].wait()
    queries = layer_norm(weight_dot(joined, sa_out_ref[...]), gains_ref[0:1, :])
    weights[2].wait()
    cross_q = rounded(weight_dot(queries + start, t2i_ref[:, :inner]))
    scale = math.log2(math.e) / math.sqrt(inner // HEADS)
    aq_ref[...] = (dot_t(by_head(cross_q).astype(BF16), t2i_ref[:, inner : 2 * inner]) * scale).astype(BF16)

    table_ref[0] = sin_y
    table_ref[1] = cos_y
    start_ref[...] = start
    queries_ref[...] = queries

    for y in range(side):
        if y * side % step == 0:
            cell_copies[y * side // step].wait()
        rows = slice(y * side, (y + 1) * side)
        e = emb_ref[rows, :].astype(F32)
        sy, cy = table_ref[0, y : y + 1, :], table_ref[1, y : y + 1, :]
        e1, e2 = e[:, :half], e[:, half:]
        keys_ref[rows, :half] = (e1 + (sin_x * cy + cos_x * sy)).astype(BF16)
        keys_ref[rows, half:] = (e2 + (cos_x * cy - sin_x * sy)).astype(BF16)

    pairs = HEADS * tokens

    def scores(at):
        return dot_t(aq_ref[...], keys_ref[pl.ds(at, SCORE_CELLS), :])

    def probabilities(at, s):
        for r0 in range(0, pairs, 16):
            rows = slice(r0, r0 + 16)
            top = top_ref[rows, :]
            total = sum_ref[rows, :]
            for k0 in range(0, SCORE_CELLS, LANES):
                p = jnp.exp2(s[rows, k0 : k0 + LANES] - top)
                total = total + p
                prob_ref[rows, pl.ds(pl.multiple_of(at + k0, LANES), LANES)] = p.astype(BF16)
            sum_ref[rows, :] = total

    def prob_step(c, carry):
        at = pl.multiple_of(c * SCORE_CELLS, SCORE_CELLS)
        probabilities(at, scores(at))
        return carry

    sum_ref[...] = jnp.zeros_like(sum_ref)
    first = scores(0)
    top_ref[...] = jnp.broadcast_to(jnp.max(first, axis=1, keepdims=True), top_ref.shape)
    probabilities(0, first)
    lax.fori_loop(1, cells // SCORE_CELLS, prob_step, 0)

    @pl.when(jnp.logical_not(jnp.max(sum_ref[...]) < LARGE_SUM))
    def _():
        top_ref[...] = jnp.full(top_ref.shape, -jnp.inf, F32)

        def top_step(c, carry):
            s = scores(pl.multiple_of(c * SCORE_CELLS, SCORE_CELLS))
            for k0 in range(0, SCORE_CELLS, LANES):
                top_ref[...] = jnp.maximum(top_ref[...], s[:, k0 : k0 + LANES])
            return carry

        lax.fori_loop(0, cells // SCORE_CELLS, top_step, 0)
        top_ref[...] = jnp.broadcast_to(jnp.max(top_ref[...], axis=1, keepdims=True), top_ref.shape)
        sum_ref[...] = jnp.zeros_like(sum_ref)
        lax.fori_loop(0, cells // SCORE_CELLS, prob_step, 0)

    @pl.when(count > 0)
    def _():
        mean_cell = dot(prob_ref[...], emb_ref[...]) / jnp.sum(sum_ref[...], axis=1, keepdims=True)
        head_out = dot(mean_cell.astype(BF16), t2i_ref[:, 2 * inner :])
        lane = lax.broadcasted_iota(jnp.int32, (tokens, inner), 1) // (inner // HEADS)
        cross_out = jnp.zeros((tokens, inner), F32)
        for h in range(HEADS):
            cross_out = jnp.where(lane == h, head_out[h * tokens : (h + 1) * tokens], cross_out)
        cross_ref[...] = cross_out

    @pl.when(count > 0)
    def _():
        for copy in weights[3:]:
            copy.wait()
        queries = layer_norm(queries_ref[...] + weight_dot(cross_ref[...], t2i_out_ref[...]), gains_ref[1:2, :])
        hidden = jnp.maximum(dot(queries.astype(BF16), up_ref[...]), 0.0)
        queries = layer_norm(queries + dot(hidden.astype(BF16), down_ref[...]), gains_ref[2:3, :])
        start = start_ref[...]
        back_k = rounded(weight_dot(queries + start, i2t_ref[:, inner : 2 * inner]))
        back_v = rounded(weight_dot(queries, i2t_ref[:, 2 * inner :]))
        hyper = rounded(weight_dot(jnp.maximum(weight_dot(queries[:slots], hyper_ref[0]), 0.0), hyper_ref[1]))
        back_ref[0] = back_k
        back_ref[1] = back_v
        hyper_out[...] = hyper

    group = slots // GROUPS
    heads = HEADS * group
    lines = heads + 2 * group
    blank = width - heads

    @pl.when(count > 0)
    def _():
        back_k, back_v, hyper = back_ref[0], back_ref[1], hyper_out[...]
        key_gap = back_k[:slots] - back_k[slots:]
        gap_scale = 0.5 / math.sqrt(inner // HEADS)
        spread = 0.5 * (back_v[:slots] - back_v[slots:])
        middle = 0.5 * (back_v[:slots] + back_v[slots:])
        b_all = rounded(centred_rows(weight_dot(middle, i2t_out_ref[...])))
        g_all = rounded(centred_rows(hyper * gains_ref[3:4, :]))
        zeros = jnp.zeros((blank, width), BF16)
        r = lax.broadcasted_iota(jnp.int32, (lines, width), 0)
        c = lax.broadcasted_iota(jnp.int32, (lines, width), 1)
        own_slot = jnp.logical_and(r % group == c % group, c < heads)
        for n in range(GROUPS):
            of = slice(n * group, (n + 1) * group)
            gap_ref[n * heads : (n + 1) * heads, :] = (
                dot_t(by_head(key_gap[of]).astype(BF16), i2t_ref[:, :inner]) * gap_scale
            ).astype(BF16)
            u = rounded(centred_rows(dot(by_head(spread[of]).astype(BF16), i2t_out_ref[...])))
            b, g = b_all[of], g_all[of]
            left = jnp.concatenate([u, 2.0 * b, g], axis=0).astype(BF16)
            right = jnp.concatenate([u.astype(BF16), zeros], axis=0)
            constant = jnp.concatenate(
                [
                    jnp.zeros((heads, 1), F32),
                    jnp.sum(b * b, axis=1, keepdims=True),
                    jnp.sum(b * g, axis=1, keepdims=True),
                ],
                axis=0,
            )
            high = rounded(constant)
            mix = jnp.where(own_slot, dot_t(left, right), 0.0)
            mix = jnp.where(c == heads, high, jnp.where(c == heads + 1, constant - high, mix))
            mix_ref[n] = mix.astype(BF16)
            row_ref[n * lines : (n + 1) * lines, :] = jnp.concatenate([2.0 * u, 2.0 * b, g], axis=0).astype(BF16)

    ones = jnp.ones((16, width), BF16)
    row_ref[GROUPS * lines :, :] = ones
    t_ref[:, heads:, :] = jnp.ones((GROUPS, blank, cells), BF16)

    out_copies = []
    for at in range(0, cells, IMAGE_CELLS):
        here = slice(at, at + IMAGE_CELLS)
        t = jnp.tanh(dot_t(gap_ref[...], keys_ref[here, :])).astype(BF16)
        for n in range(GROUPS):
            t_ref[n, :heads, here] = t[n * heads : (n + 1) * heads]
        cell_part = dot_t(row_ref[...], emb_ref[here, :])
        sums = cell_part[GROUPS * lines : GROUPS * lines + 8]
        e = emb_ref[here, :].astype(F32)
        squares = jnp.concatenate(halves(e[:, :half] * e[:, :half] + e[:, half:] * e[:, half:]), axis=1)
        own = dot_t(ones, squares)[:8] - sums * sums * (1.0 / width)
        logits = []
        for n in range(GROUPS):
            line = cell_part[n * lines : (n + 1) * lines] + dot(mix_ref[n], t_ref[n, :, here])
            t32 = t[n * heads : (n + 1) * heads].astype(F32)
            var = line[heads : heads + group] + jnp.concatenate([own] * (group // 8), axis=0)
            for h in range(HEADS):
                var = var + t32[h * group : (h + 1) * group] * line[h * group : (h + 1) * group]
            var = jnp.maximum(var, 0.0)
            logits.append(line[heads + group :] * lax.rsqrt(var + EPS * width))
        logit = rounded(jnp.concatenate(logits, axis=0))
        live = lax.broadcasted_iota(jnp.int32, logit.shape, 0) < count
        masked = jnp.where(live, logit, 0.0)
        logits_ref[:, here] = masked.astype(BF16)
        out_copies.append(pltpu.make_async_copy(logits_ref.at[:, here], logits_hbm.at[:, here], out_sem.at[at // IMAGE_CELLS]))
        out_copies[-1].start()
        cover = jnp.sum(jnp.where(live, jax.nn.sigmoid(masked), 0.0), axis=0, keepdims=True)
        for k0 in range(0, IMAGE_CELLS, side):
            cov_ref[(at + k0) // side : (at + k0) // side + 1, :] = cover[:, k0 : k0 + side]
    cov = cov_ref[...]
    tail_ref[...] = jnp.concatenate([cov[:, side - SEAM :], cov[:, : side - SEAM]], axis=1)
    for copy in out_copies:
        copy.wait()


def seam_kernel(n, cov_hbm, tail_hbm, left_hbm, right_hbm, zero_ref, send_sem, recv_sem, zero_sem):
    me = lax.axis_index("col")
    has_left, has_right = me > 0, me < n - 1
    barrier = pltpu.get_barrier_semaphore()
    mesh_id = pl.DeviceIdType.MESH

    def to_left():
        return pltpu.make_async_remote_copy(
            src_ref=cov_hbm,
            dst_ref=right_hbm,
            send_sem=send_sem.at[0],
            recv_sem=recv_sem.at[0],
            device_id={"col": me - 1},
            device_id_type=mesh_id,
        )

    def to_right():
        return pltpu.make_async_remote_copy(
            src_ref=tail_hbm,
            dst_ref=left_hbm,
            send_sem=send_sem.at[1],
            recv_sem=recv_sem.at[1],
            device_id={"col": me + 1},
            device_id_type=mesh_id,
        )

    @pl.when(has_left)
    def _():
        pl.semaphore_signal(barrier, inc=1, device_id={"col": me - 1}, device_id_type=mesh_id)

    @pl.when(has_right)
    def _():
        pl.semaphore_signal(barrier, inc=1, device_id={"col": me + 1}, device_id_type=mesh_id)

    pl.semaphore_wait(barrier, has_left.astype(jnp.int32) + has_right.astype(jnp.int32))

    @pl.when(has_left)
    def _():
        to_left().start()

    @pl.when(has_right)
    def _():
        to_right().start()

    @pl.when(jnp.logical_not(has_left))
    def _():
        zero_ref[...] = jnp.zeros_like(zero_ref)
        copy = pltpu.make_async_copy(zero_ref, left_hbm, zero_sem)
        copy.start()
        copy.wait()

    @pl.when(jnp.logical_not(has_right))
    def _():
        zero_ref[...] = jnp.zeros_like(zero_ref)
        copy = pltpu.make_async_copy(zero_ref, right_hbm, zero_sem)
        copy.start()
        copy.wait()

    @pl.when(has_right)
    def _():
        to_right().wait_send()
        to_left().wait_recv()

    @pl.when(has_left)
    def _():
        to_left().wait_send()
        to_right().wait_recv()


def tile_call(counts, emb, points, gauss, prompt, mask, sa_qkv, sa_out, t2i, t2i_out, up, down, i2t, i2t_out, hyper, gains):
    cells, width = emb.shape
    slots = points.shape[1]
    rows = 2 * slots * HEADS
    heads = HEADS * slots // GROUPS
    lines = heads + 2 * slots // GROUPS
    vmem = pl.BlockSpec(memory_space=pltpu.VMEM)
    hbm = pl.BlockSpec(memory_space=pl.ANY)
    large = [emb, sa_qkv, sa_out, t2i, t2i_out, up, down, i2t, i2t_out, hyper]
    return pl.pallas_call(
        tile_kernel,
        out_shape=(
            jax.ShapeDtypeStruct((slots, cells), BF16),
            jax.ShapeDtypeStruct((math.isqrt(cells),) * 2, F32),
            jax.ShapeDtypeStruct((math.isqrt(cells),) * 2, F32),
        ),
        in_specs=[pl.BlockSpec(memory_space=pltpu.SMEM)] + [vmem] * 5 + [hbm] * len(large),
        out_specs=(hbm, vmem, vmem),
        scratch_shapes=[pltpu.VMEM(a.shape, a.dtype) for a in large]
        + [
            pltpu.VMEM((slots, cells), BF16),
            pltpu.VMEM((cells, width), BF16),
            pltpu.VMEM((rows, cells), BF16),
            pltpu.VMEM((rows, width), BF16),
            pltpu.VMEM((rows, LANES), F32),
            pltpu.VMEM((rows, LANES), F32),
            pltpu.VMEM((2 * slots, width), F32),
            pltpu.VMEM((2 * slots, width), F32),
            pltpu.VMEM((2 * slots, t2i.shape[1] // 3), F32),
            pltpu.VMEM((2, 2 * slots, t2i.shape[1] // 3), F32),
            pltpu.VMEM((slots, width), F32),
            pltpu.VMEM((GROUPS * heads, width), BF16),
            pltpu.VMEM((GROUPS * lines + 16, width), BF16),
            pltpu.VMEM((GROUPS, lines, width), BF16),
            pltpu.VMEM((GROUPS, width, cells), BF16),
            pltpu.VMEM((2, math.isqrt(cells), width // 2), F32),
            pltpu.SemaphoreType.DMA((len(large) - 1,)),
            pltpu.SemaphoreType.DMA((EMB_COPIES,)),
            pltpu.SemaphoreType.DMA((cells // IMAGE_CELLS,)),
        ],
        compiler_params=pltpu.CompilerParams(vmem_limit_bytes=58 * 2**20),
        name="tile",
    )(counts, points, gauss, prompt, mask, gains, *large)


def seam_call(cov, tail, n):
    hbm = pl.BlockSpec(memory_space=pl.ANY)
    return pl.pallas_call(
        functools.partial(seam_kernel, n),
        out_shape=(jax.ShapeDtypeStruct(cov.shape, F32), jax.ShapeDtypeStruct(cov.shape, F32)),
        in_specs=[hbm, hbm],
        out_specs=(hbm, hbm),
        scratch_shapes=[
            pltpu.VMEM(cov.shape, F32),
            pltpu.SemaphoreType.DMA((2,)),
            pltpu.SemaphoreType.DMA((2,)),
            pltpu.SemaphoreType.DMA(()),
        ],
        compiler_params=pltpu.CompilerParams(collective_id=0, has_side_effects=True),
        name="seam",
    )(cov, tail)


def blend(left, cov, right):
    side = cov.shape[1]
    padded = jnp.concatenate([left[:, :SEAM], cov, right[:, :SEAM]], axis=1)
    blended = jnp.zeros_like(cov)
    for offset in range(-SEAM, SEAM + 1):
        factor = (SEAM + 1 - abs(offset)) / (SEAM + 1) ** 2
        blended = blended + factor * padded[:, SEAM + offset : SEAM + offset + side]
    return blended


def shards(
    embedding,
    counts,
    points,
    pe_gauss,
    point_embed,
    mask_token,
    sa_qkv,
    sa_out,
    t2i_qkv,
    t2i_out,
    mlp_up,
    mlp_down,
    i2t_qkv,
    i2t_out,
    hyper_w,
    ln_gains,
):
    side, _, width = embedding.shape
    logits, cov, tail = tile_call(
        counts,
        embedding.reshape(side * side, width),
        points[0, 0],
        pe_gauss,
        point_embed.reshape(1, width),
        mask_token.reshape(1, width),
        sa_qkv,
        sa_out,
        t2i_qkv,
        t2i_out,
        mlp_up,
        mlp_down,
        i2t_qkv,
        i2t_out,
        hyper_w,
        ln_gains,
    )
    left, right = seam_call(cov, tail, lax.axis_size("col"))
    blended = blend(left, cov, right)
    return logits.reshape(1, 1, *logits.shape), blended


def solution(mesh):
    whole = [P()] * 13
    return jax.shard_map(
        shards,
        mesh=mesh,
        in_specs=(P("row", "col", None), P("col", None), P("row", "col", None, None), *whole),
        out_specs=(P("row", "col", None, None), P("row", "col")),
        check_vma=False,
    )
```

```python
import functools
import math

import jax
import jax.numpy as jnp
import numpy as np
from jax import lax
from jax.experimental import pallas as pl
from jax.experimental.pallas import tpu as pltpu
from jax.sharding import PartitionSpec as P

HEADS = 8
SEAM = 4
IMG = 1024
EPS = 1e-05
F32 = jnp.float32
BF16 = jnp.bfloat16
LANES = 128
GROUPS = 2
EMB_COPIES = 4
SCORE_CELLS = 1024
LARGE_SUM = 2.0**100
IMAGE_CELLS = 512


def turn_polynomials():
    z = np.linspace(0.0, 0.25, 4001)[1:]
    r = np.sqrt(z)
    fit = np.polynomial.chebyshev.Chebyshev.fit
    power = lambda c: [float(v) for v in c.convert(kind=np.polynomial.Polynomial, domain=[-1, 1]).coef]
    return (
        power(fit(z, np.sin(2 * math.pi * r) / r, 8, domain=[0.0, 0.25])),
        power(fit(z, np.cos(2 * math.pi * r), 8, domain=[0.0, 0.25])),
    )


SIN_COEF, COS_COEF = turn_polynomials()


def sin_cos_turns(turns):
    r = turns - jnp.floor(turns + 0.5)
    z = r * r
    s = jnp.full_like(z, SIN_COEF[-1])
    c = jnp.full_like(z, COS_COEF[-1])
    for a, b in zip(SIN_COEF[-2::-1], COS_COEF[-2::-1]):
        s = s * z + a
        c = c * z + b
    return s * r, c


def dot(a, b):
    return lax.dot_general(a, b, (((1,), (0,)), ((), ())), preferred_element_type=F32)


def dot_t(a, b):
    return lax.dot_general(a, b, (((1,), (1,)), ((), ())), preferred_element_type=F32)


def halves(values):
    high = values.astype(BF16)
    return high, (values - high.astype(F32)).astype(BF16)


def weight_dot(values, weight):
    rows = values.shape[0]
    both = dot(jnp.concatenate(halves(values), axis=0), weight)
    return both[:rows] + both[rows:]


def layer_norm(values, gain):
    centred = values - jnp.mean(values, axis=-1, keepdims=True)
    var = jnp.mean(centred * centred, axis=-1, keepdims=True)
    return centred * lax.rsqrt(var + EPS) * gain


def rounded(values):
    return values.astype(BF16).astype(F32)


def by_head(values):
    lane = lax.broadcasted_iota(jnp.int32, values.shape, 1) // (values.shape[1] // HEADS)
    return jnp.concatenate([jnp.where(lane == h, values, 0.0) for h in range(HEADS)], axis=0)


def centred_rows(values):
    return values - jnp.mean(values, axis=-1, keepdims=True)


def as_column(row):
    n = row.shape[1]
    i = lax.broadcasted_iota(jnp.int32, (n, n), 0)
    j = lax.broadcasted_iota(jnp.int32, (n, n), 1)
    return jnp.sum(jnp.where(i == j, jnp.broadcast_to(row, (n, n)), 0.0), axis=1, keepdims=True)


def tile_kernel(
    counts_ref,
    points_ref,
    gauss_ref,
    prompt_ref,
    mask_ref,
    gains_ref,
    emb_hbm,
    sa_qkv_hbm,
    sa_out_hbm,
    t2i_hbm,
    t2i_out_hbm,
    up_hbm,
    down_hbm,
    i2t_hbm,
    i2t_out_hbm,
    hyper_hbm,
    logits_hbm,
    cov_ref,
    emb_ref,
    sa_qkv_ref,
    sa_out_ref,
    t2i_ref,
    t2i_out_ref,
    up_ref,
    down_ref,
    i2t_ref,
    i2t_out_ref,
    hyper_ref,
    logits_ref,
    keys_ref,
    prob_ref,
    aq_ref,
    top_ref,
    sum_ref,
    start_ref,
    queries_ref,
    cross_ref,
    back_ref,
    hyper_out,
    gap_ref,
    row_ref,
    mix_ref,
    t_ref,
    table_ref,
    in_sem,
    emb_sem,
    out_sem,
):
    cells, width = emb_ref.shape
    slots = points_ref.shape[1]
    tokens = 2 * slots
    half = width // 2
    inner = t2i_ref.shape[1] // 3
    side = math.isqrt(cells)
    count = counts_ref[0, lax.axis_index("row")]

    weights = [
        pltpu.make_async_copy(source, target, in_sem.at[i])
        for i, (source, target) in enumerate(
            [
                (sa_qkv_hbm, sa_qkv_ref),
                (sa_out_hbm, sa_out_ref),
                (t2i_hbm, t2i_ref),
                (t2i_out_hbm, t2i_out_ref),
                (up_hbm, up_ref),
                (down_hbm, down_ref),
                (i2t_hbm, i2t_ref),
                (hyper_hbm, hyper_ref),
                (i2t_out_hbm, i2t_out_ref),
            ]
        )
    ]
    step = cells // EMB_COPIES
    cell_copies = [
        pltpu.make_async_copy(emb_hbm.at[pl.ds(i * step, step)], emb_ref.at[pl.ds(i * step, step)], emb_sem.at[i])
        for i in range(EMB_COPIES)
    ]
    for copy in weights[:3] + cell_copies + weights[3:]:
        copy.start()

    steps = (2.0 * (lax.broadcasted_iota(jnp.int32, (side, half), 0).astype(F32) + 0.5)) / side - 1.0
    sin_x, cos_x = sin_cos_turns(steps * gauss_ref[0:1, :])
    sin_y, cos_y = sin_cos_turns(steps * gauss_ref[1:2, :])

    coords = (2.0 * (points_ref[...].astype(F32) + 0.5)) / IMG - 1.0
    turns = as_column(coords[0:1, :]) * gauss_ref[0:1, :] + as_column(coords[1:2, :]) * gauss_ref[1:2, :]
    sin_p, cos_p = sin_cos_turns(turns)
    prompt = jnp.concatenate([sin_p, cos_p], axis=1) + prompt_ref[...]
    start = jnp.concatenate([jnp.broadcast_to(mask_ref[...], (slots, width)), prompt], axis=0)
    weights[0].wait()
    qkv = weight_dot(start, sa_qkv_ref[...])
    q, k, v = qkv[:, :width], qkv[:, width : 2 * width], qkv[:, 2 * width :]
    k_gap = k[slots:] - k[:slots]
    v_gap = v[slots:] - v[:slots]
    self_width = width // HEADS
    i = lax.broadcasted_iota(jnp.int32, (width, width), 0) // self_width
    j = lax.broadcasted_iota(jnp.int32, (width, width), 1) // self_width
    same = jnp.where(i == j, 1.0, 0.0).astype(BF16)
    gap = weight_dot(q * jnp.concatenate([k_gap, k_gap], axis=0), same) / math.sqrt(self_width)
    second = jax.nn.sigmoid(gap)
    joined = jnp.concatenate([v[:slots], v[:slots]], axis=0) + second * jnp.concatenate([v_gap, v_gap], axis=0)
    weights[1].wait()
    queries = layer_norm(weight_dot(joined, sa_out_ref[...]), gains_ref[0:1, :])
    weights[2].wait()
    cross_q = rounded(weight_dot(queries + start, t2i_ref[:, :inner]))
    scale = math.log2(math.e) / math.sqrt(inner // HEADS)
    aq_ref[...] = (dot_t(by_head(cross_q).astype(BF16), t2i_ref[:, inner : 2 * inner]) * scale).astype(BF16)

    table_ref[0] = sin_y
    table_ref[1] = cos_y
    start_ref[...] = start
    queries_ref[...] = queries

    for y in range(side):
        if y * side % step == 0:
            cell_copies[y * side // step].wait()
        rows = slice(y * side, (y + 1) * side)
        e = emb_ref[rows, :].astype(F32)
        sy, cy = table_ref[0, y : y + 1, :], table_ref[1, y : y + 1, :]
        e1, e2 = e[:, :half], e[:, half:]
        keys_ref[rows, :half] = (e1 + (sin_x * cy + cos_x * sy)).astype(BF16)
        keys_ref[rows, half:] = (e2 + (cos_x * cy - sin_x * sy)).astype(BF16)

    pairs = HEADS * tokens

    def scores(at):
        return dot_t(aq_ref[...], keys_ref[pl.ds(at, SCORE_CELLS), :])

    def probabilities(at, s):
        for r0 in range(0, pairs, 16):
            rows = slice(r0, r0 + 16)
            top = top_ref[rows, :]
            total = sum_ref[rows, :]
            for k0 in range(0, SCORE_CELLS, LANES):
                p = jnp.exp2(s[rows, k0 : k0 + LANES] - top)
                total = total + p
                prob_ref[rows, pl.ds(pl.multiple_of(at + k0, LANES), LANES)] = p.astype(BF16)
            sum_ref[rows, :] = total

    def prob_step(c, carry):
        at = pl.multiple_of(c * SCORE_CELLS, SCORE_CELLS)
        probabilities(at, scores(at))
        return carry

    sum_ref[...] = jnp.zeros_like(sum_ref)
    first = scores(0)
    top_ref[...] = jnp.broadcast_to(jnp.max(first, axis=1, keepdims=True), top_ref.shape)
    probabilities(0, first)
    lax.fori_loop(1, cells // SCORE_CELLS, prob_step, 0)

    @pl.when(jnp.logical_not(jnp.max(sum_ref[...]) < LARGE_SUM))
    def _():
        top_ref[...] = jnp.full(top_ref.shape, -jnp.inf, F32)

        def top_step(c, carry):
            s = scores(pl.multiple_of(c * SCORE_CELLS, SCORE_CELLS))
            for k0 in range(0, SCORE_CELLS, LANES):
                top_ref[...] = jnp.maximum(top_ref[...], s[:, k0 : k0 + LANES])
            return carry

        lax.fori_loop(0, cells // SCORE_CELLS, top_step, 0)
        top_ref[...] = jnp.broadcast_to(jnp.max(top_ref[...], axis=1, keepdims=True), top_ref.shape)
        sum_ref[...] = jnp.zeros_like(sum_ref)
        lax.fori_loop(0, cells // SCORE_CELLS, prob_step, 0)

    @pl.when(count > 0)
    def _():
        mean_cell = dot(prob_ref[...], emb_ref[...]) / jnp.sum(sum_ref[...], axis=1, keepdims=True)
        head_out = dot(mean_cell.astype(BF16), t2i_ref[:, 2 * inner :])
        lane = lax.broadcasted_iota(jnp.int32, (tokens, inner), 1) // (inner // HEADS)
        cross_out = jnp.zeros((tokens, inner), F32)
        for h in range(HEADS):
            cross_out = jnp.where(lane == h, head_out[h * tokens : (h + 1) * tokens], cross_out)
        cross_ref[...] = cross_out

    @pl.when(count > 0)
    def _():
        for copy in weights[3:]:
            copy.wait()
        queries = layer_norm(queries_ref[...] + weight_dot(cross_ref[...], t2i_out_ref[...]), gains_ref[1:2, :])
        hidden = jnp.maximum(dot(queries.astype(BF16), up_ref[...]), 0.0)
        queries = layer_norm(queries + dot(hidden.astype(BF16), down_ref[...]), gains_ref[2:3, :])
        start = start_ref[...]
        back_k = rounded(weight_dot(queries + start, i2t_ref[:, inner : 2 * inner]))
        back_v = rounded(weight_dot(queries, i2t_ref[:, 2 * inner :]))
        hyper = rounded(weight_dot(jnp.maximum(weight_dot(queries[:slots], hyper_ref[0]), 0.0), hyper_ref[1]))
        back_ref[0] = back_k
        back_ref[1] = back_v
        hyper_out[...] = hyper

    group = slots // GROUPS
    heads = HEADS * group
    lines = heads + 2 * group
    blank = width - heads

    @pl.when(count > 0)
    def _():
        back_k, back_v, hyper = back_ref[0], back_ref[1], hyper_out[...]
        key_gap = back_k[:slots] - back_k[slots:]
        gap_scale = 0.5 / math.sqrt(inner // HEADS)
        spread = 0.5 * (back_v[:slots] - back_v[slots:])
        middle = 0.5 * (back_v[:slots] + back_v[slots:])
        b_all = rounded(centred_rows(weight_dot(middle, i2t_out_ref[...])))
        g_all = rounded(centred_rows(hyper * gains_ref[3:4, :]))
        zeros = jnp.zeros((blank, width), BF16)
        r = lax.broadcasted_iota(jnp.int32, (lines, width), 0)
        c = lax.broadcasted_iota(jnp.int32, (lines, width), 1)
        own_slot = jnp.logical_and(r % group == c % group, c < heads)
        for n in range(GROUPS):
            of = slice(n * group, (n + 1) * group)
            gap_ref[n * heads : (n + 1) * heads, :] = (
                dot_t(by_head(key_gap[of]).astype(BF16), i2t_ref[:, :inner]) * gap_scale
            ).astype(BF16)
            u = rounded(centred_rows(dot(by_head(spread[of]).astype(BF16), i2t_out_ref[...])))
            b, g = b_all[of], g_all[of]
            left = jnp.concatenate([u, 2.0 * b, g], axis=0).astype(BF16)
            right = jnp.concatenate([u.astype(BF16), zeros], axis=0)
            constant = jnp.concatenate(
                [
                    jnp.zeros((heads, 1), F32),
                    jnp.sum(b * b, axis=1, keepdims=True),
                    jnp.sum(b * g, axis=1, keepdims=True),
                ],
                axis=0,
            )
            high = rounded(constant)
            mix = jnp.where(own_slot, dot_t(left, right), 0.0)
            mix = jnp.where(c == heads, high, jnp.where(c == heads + 1, constant - high, mix))
            mix_ref[n] = mix.astype(BF16)
            row_ref[n * lines : (n + 1) * lines, :] = jnp.concatenate([2.0 * u, 2.0 * b, g], axis=0).astype(BF16)

    ones = jnp.ones((16, width), BF16)
    row_ref[GROUPS * lines :, :] = ones
    t_ref[:, heads:, :] = jnp.ones((GROUPS, blank, cells), BF16)

    out_copies = []
    for at in range(0, cells, IMAGE_CELLS):
        here = slice(at, at + IMAGE_CELLS)
        t = jnp.tanh(dot_t(gap_ref[...], keys_ref[here, :])).astype(BF16)
        for n in range(GROUPS):
            t_ref[n, :heads, here] = t[n * heads : (n + 1) * heads]
        cell_part = dot_t(row_ref[...], emb_ref[here, :])
        sums = cell_part[GROUPS * lines : GROUPS * lines + 8]
        e = emb_ref[here, :].astype(F32)
        squares = jnp.concatenate(halves(e[:, :half] * e[:, :half] + e[:, half:] * e[:, half:]), axis=1)
        own = dot_t(ones, squares)[:8] - sums * sums * (1.0 / width)
        logits = []
        for n in range(GROUPS):
            line = cell_part[n * lines : (n + 1) * lines] + dot(mix_ref[n], t_ref[n, :, here])
            t32 = t[n * heads : (n + 1) * heads].astype(F32)
            var = line[heads : heads + group] + jnp.concatenate([own] * (group // 8), axis=0)
            for h in range(HEADS):
                var = var + t32[h * group : (h + 1) * group] * line[h * group : (h + 1) * group]
            var = jnp.maximum(var, 0.0)
            logits.append(line[heads + group :] * lax.rsqrt(var + EPS * width))
        logit = rounded(jnp.concatenate(logits, axis=0))
        live = lax.broadcasted_iota(jnp.int32, logit.shape, 0) < count
        masked = jnp.where(live, logit, 0.0)
        logits_ref[:, here] = masked.astype(BF16)
        out_copies.append(pltpu.make_async_copy(logits_ref.at[:, here], logits_hbm.at[:, here], out_sem.at[at // IMAGE_CELLS]))
        out_copies[-1].start()
        cover = jnp.sum(jnp.where(live, jax.nn.sigmoid(masked), 0.0), axis=0, keepdims=True)
        for k0 in range(0, IMAGE_CELLS, LANES):
            cov_ref[(at + k0) // LANES : (at + k0) // LANES + 1, :] = cover[:, k0 : k0 + LANES]
    for copy in out_copies:
        copy.wait()


def seam_kernel(n, cov_hbm, left_hbm, right_hbm, zero_ref, send_sem, recv_sem, zero_sem):
    me = lax.axis_index("col")
    has_left, has_right = me > 0, me < n - 1
    barrier = pltpu.get_barrier_semaphore()
    mesh_id = pl.DeviceIdType.MESH

    def to_left():
        return pltpu.make_async_remote_copy(
            src_ref=cov_hbm,
            dst_ref=right_hbm,
            send_sem=send_sem.at[0],
            recv_sem=recv_sem.at[0],
            device_id={"col": me - 1},
            device_id_type=mesh_id,
        )

    def to_right():
        return pltpu.make_async_remote_copy(
            src_ref=cov_hbm,
            dst_ref=left_hbm,
            send_sem=send_sem.at[1],
            recv_sem=recv_sem.at[1],
            device_id={"col": me + 1},
            device_id_type=mesh_id,
        )

    @pl.when(has_left)
    def _():
        pl.semaphore_signal(barrier, inc=1, device_id={"col": me - 1}, device_id_type=mesh_id)

    @pl.when(has_right)
    def _():
        pl.semaphore_signal(barrier, inc=1, device_id={"col": me + 1}, device_id_type=mesh_id)

    pl.semaphore_wait(barrier, has_left.astype(jnp.int32) + has_right.astype(jnp.int32))

    @pl.when(has_left)
    def _():
        to_left().start()

    @pl.when(has_right)
    def _():
        to_right().start()

    @pl.when(jnp.logical_not(has_left))
    def _():
        zero_ref[...] = jnp.zeros_like(zero_ref)
        copy = pltpu.make_async_copy(zero_ref, left_hbm, zero_sem)
        copy.start()
        copy.wait()

    @pl.when(jnp.logical_not(has_right))
    def _():
        zero_ref[...] = jnp.zeros_like(zero_ref)
        copy = pltpu.make_async_copy(zero_ref, right_hbm, zero_sem)
        copy.start()
        copy.wait()

    @pl.when(has_right)
    def _():
        to_right().wait_send()
        to_left().wait_recv()

    @pl.when(has_left)
    def _():
        to_left().wait_send()
        to_right().wait_recv()


def tile_call(counts, emb, points, gauss, prompt, mask, sa_qkv, sa_out, t2i, t2i_out, up, down, i2t, i2t_out, hyper, gains):
    cells, width = emb.shape
    slots = points.shape[1]
    rows = 2 * slots * HEADS
    heads = HEADS * slots // GROUPS
    lines = heads + 2 * slots // GROUPS
    vmem = pl.BlockSpec(memory_space=pltpu.VMEM)
    hbm = pl.BlockSpec(memory_space=pl.ANY)
    large = [emb, sa_qkv, sa_out, t2i, t2i_out, up, down, i2t, i2t_out, hyper]
    return pl.pallas_call(
        tile_kernel,
        out_shape=(
            jax.ShapeDtypeStruct((slots, cells), BF16),
            jax.ShapeDtypeStruct((cells // LANES, LANES), F32),
        ),
        in_specs=[pl.BlockSpec(memory_space=pltpu.SMEM)] + [vmem] * 5 + [hbm] * len(large),
        out_specs=(hbm, vmem),
        scratch_shapes=[pltpu.VMEM(a.shape, a.dtype) for a in large]
        + [
            pltpu.VMEM((slots, cells), BF16),
            pltpu.VMEM((cells, width), BF16),
            pltpu.VMEM((rows, cells), BF16),
            pltpu.VMEM((rows, width), BF16),
            pltpu.VMEM((rows, LANES), F32),
            pltpu.VMEM((rows, LANES), F32),
            pltpu.VMEM((2 * slots, width), F32),
            pltpu.VMEM((2 * slots, width), F32),
            pltpu.VMEM((2 * slots, t2i.shape[1] // 3), F32),
            pltpu.VMEM((2, 2 * slots, t2i.shape[1] // 3), F32),
            pltpu.VMEM((slots, width), F32),
            pltpu.VMEM((GROUPS * heads, width), BF16),
            pltpu.VMEM((GROUPS * lines + 16, width), BF16),
            pltpu.VMEM((GROUPS, lines, width), BF16),
            pltpu.VMEM((GROUPS, width, cells), BF16),
            pltpu.VMEM((2, math.isqrt(cells), width // 2), F32),
            pltpu.SemaphoreType.DMA((len(large) - 1,)),
            pltpu.SemaphoreType.DMA((EMB_COPIES,)),
            pltpu.SemaphoreType.DMA((cells // IMAGE_CELLS,)),
        ],
        compiler_params=pltpu.CompilerParams(vmem_limit_bytes=58 * 2**20),
        name="tile",
    )(counts, points, gauss, prompt, mask, gains, *large)


def seam_call(cov, n):
    hbm = pl.BlockSpec(memory_space=pl.ANY)
    return pl.pallas_call(
        functools.partial(seam_kernel, n),
        out_shape=(jax.ShapeDtypeStruct(cov.shape, F32), jax.ShapeDtypeStruct(cov.shape, F32)),
        in_specs=[hbm],
        out_specs=(hbm, hbm),
        scratch_shapes=[
            pltpu.VMEM(cov.shape, F32),
            pltpu.SemaphoreType.DMA((2,)),
            pltpu.SemaphoreType.DMA((2,)),
            pltpu.SemaphoreType.DMA(()),
        ],
        compiler_params=pltpu.CompilerParams(collective_id=0, has_side_effects=True),
        name="seam",
    )(cov)


def blend_kernel(left_ref, cov_ref, right_ref, out_ref):
    side = out_ref.shape[0]
    left, cov, right = left_ref[...], cov_ref[...], right_ref[...]
    x = lax.broadcasted_iota(jnp.int32, cov.shape, 1) % side
    total = (SEAM + 1.0) * cov
    for d in range(1, SEAM + 1):
        after = jnp.where(x < side - d, pltpu.roll(cov, LANES - d, 1), pltpu.roll(right, side - d, 1))
        before = jnp.where(x >= d, pltpu.roll(cov, d, 1), pltpu.roll(left, side + d, 1))
        total = total + (SEAM + 1.0 - d) * (after + before)
    total = total * (1.0 / (SEAM + 1) ** 2)
    out_ref[pl.ds(0, side // 2, stride=2), :] = total[:, :side]
    out_ref[pl.ds(1, side // 2, stride=2), :] = total[:, side:]


def blend(left, cov, right, side):
    vmem = pl.BlockSpec(memory_space=pltpu.VMEM)
    return pl.pallas_call(
        blend_kernel,
        out_shape=jax.ShapeDtypeStruct((side, side), F32),
        in_specs=[vmem] * 3,
        out_specs=vmem,
        name="blend",
    )(left, cov, right)


def shards(
    embedding,
    counts,
    points,
    pe_gauss,
    point_embed,
    mask_token,
    sa_qkv,
    sa_out,
    t2i_qkv,
    t2i_out,
    mlp_up,
    mlp_down,
    i2t_qkv,
    i2t_out,
    hyper_w,
    ln_gains,
):
    side, _, width = embedding.shape
    logits, cov = tile_call(
        counts,
        embedding.reshape(side * side, width),
        points[0, 0],
        pe_gauss,
        point_embed.reshape(1, width),
        mask_token.reshape(1, width),
        sa_qkv,
        sa_out,
        t2i_qkv,
        t2i_out,
        mlp_up,
        mlp_down,
        i2t_qkv,
        i2t_out,
        hyper_w,
        ln_gains,
    )
    left, right = seam_call(cov, lax.axis_size("col"))
    blended = blend(left, cov, right, side)
    return logits.reshape(1, 1, *logits.shape), blended


def solution(mesh):
    whole = [P()] * 13
    return jax.shard_map(
        shards,
        mesh=mesh,
        in_specs=(P("row", "col", None), P("col", None), P("row", "col", None, None), *whole),
        out_specs=(P("row", "col", None, None), P("row", "col")),
        check_vma=False,
    )
```

```python
import functools
import math

import jax
import jax.numpy as jnp
import numpy as np
from jax import lax
from jax.experimental import pallas as pl
from jax.experimental.pallas import tpu as pltpu
from jax.sharding import PartitionSpec as P

HEADS = 8
SEAM = 4
IMG = 1024
EPS = 1e-05
F32 = jnp.float32
BF16 = jnp.bfloat16
LANES = 128
GROUPS = 2
EMB_COPIES = 4
SCORE_CELLS = 1024
LARGE_SUM = 2.0**100
IMAGE_CELLS = 512


def turn_polynomials():
    z = np.linspace(0.0, 0.25, 4001)[1:]
    r = np.sqrt(z)
    fit = np.polynomial.chebyshev.Chebyshev.fit
    power = lambda c: [float(v) for v in c.convert(kind=np.polynomial.Polynomial, domain=[-1, 1]).coef]
    return (
        power(fit(z, np.sin(2 * math.pi * r) / r, 8, domain=[0.0, 0.25])),
        power(fit(z, np.cos(2 * math.pi * r), 8, domain=[0.0, 0.25])),
    )


SIN_COEF, COS_COEF = turn_polynomials()


def sin_cos_turns(turns):
    r = turns - jnp.floor(turns + 0.5)
    z = r * r
    s = jnp.full_like(z, SIN_COEF[-1])
    c = jnp.full_like(z, COS_COEF[-1])
    for a, b in zip(SIN_COEF[-2::-1], COS_COEF[-2::-1]):
        s = s * z + a
        c = c * z + b
    return s * r, c


def dot(a, b):
    return lax.dot_general(a, b, (((1,), (0,)), ((), ())), preferred_element_type=F32)


def dot_t(a, b):
    return lax.dot_general(a, b, (((1,), (1,)), ((), ())), preferred_element_type=F32)


def halves(values):
    high = values.astype(BF16)
    return high, (values - high.astype(F32)).astype(BF16)


def weight_dot(values, weight):
    rows = values.shape[0]
    both = dot(jnp.concatenate(halves(values), axis=0), weight)
    return both[:rows] + both[rows:]


def layer_norm(values, gain):
    centred = values - jnp.mean(values, axis=-1, keepdims=True)
    var = jnp.mean(centred * centred, axis=-1, keepdims=True)
    return centred * lax.rsqrt(var + EPS) * gain


def rounded(values):
    return values.astype(BF16).astype(F32)


def by_head(values):
    lane = lax.broadcasted_iota(jnp.int32, values.shape, 1) // (values.shape[1] // HEADS)
    return jnp.concatenate([jnp.where(lane == h, values, 0.0) for h in range(HEADS)], axis=0)


def centred_rows(values):
    return values - jnp.mean(values, axis=-1, keepdims=True)


def as_column(row):
    n = row.shape[1]
    i = lax.broadcasted_iota(jnp.int32, (n, n), 0)
    j = lax.broadcasted_iota(jnp.int32, (n, n), 1)
    return jnp.sum(jnp.where(i == j, jnp.broadcast_to(row, (n, n)), 0.0), axis=1, keepdims=True)


def tile_kernel(
    counts_ref,
    points_ref,
    gauss_ref,
    prompt_ref,
    mask_ref,
    gains_ref,
    emb_hbm,
    sa_qkv_hbm,
    sa_out_hbm,
    t2i_hbm,
    t2i_out_hbm,
    up_hbm,
    down_hbm,
    i2t_hbm,
    i2t_out_hbm,
    hyper_hbm,
    logits_hbm,
    cov_hbm,
    emb_ref,
    sa_qkv_ref,
    sa_out_ref,
    t2i_ref,
    t2i_out_ref,
    up_ref,
    down_ref,
    i2t_ref,
    i2t_out_ref,
    hyper_ref,
    logits_ref,
    keys_ref,
    prob_ref,
    aq_ref,
    top_ref,
    sum_ref,
    start_ref,
    queries_ref,
    cross_ref,
    back_ref,
    hyper_out,
    gap_ref,
    row_ref,
    mix_ref,
    t_ref,
    table_ref,
    in_sem,
    emb_sem,
    out_sem,
    cov_ref,
    cov_sem,
):
    cells, width = emb_ref.shape
    slots = points_ref.shape[1]
    tokens = 2 * slots
    half = width // 2
    inner = t2i_ref.shape[1] // 3
    side = math.isqrt(cells)
    count = counts_ref[0, lax.axis_index("row")]

    weights = [
        pltpu.make_async_copy(source, target, in_sem.at[i])
        for i, (source, target) in enumerate(
            [
                (sa_qkv_hbm, sa_qkv_ref),
                (sa_out_hbm, sa_out_ref),
                (t2i_hbm, t2i_ref),
                (t2i_out_hbm, t2i_out_ref),
                (up_hbm, up_ref),
                (down_hbm, down_ref),
                (i2t_hbm, i2t_ref),
                (hyper_hbm, hyper_ref),
                (i2t_out_hbm, i2t_out_ref),
            ]
        )
    ]
    step = cells // EMB_COPIES
    cell_copies = [
        pltpu.make_async_copy(emb_hbm.at[pl.ds(i * step, step)], emb_ref.at[pl.ds(i * step, step)], emb_sem.at[i])
        for i in range(EMB_COPIES)
    ]
    for copy in weights[:3] + cell_copies + weights[3:]:
        copy.start()

    steps = (2.0 * (lax.broadcasted_iota(jnp.int32, (side, half), 0).astype(F32) + 0.5)) / side - 1.0
    sin_x, cos_x = sin_cos_turns(steps * gauss_ref[0:1, :])
    sin_y, cos_y = sin_cos_turns(steps * gauss_ref[1:2, :])

    coords = (2.0 * (points_ref[...].astype(F32) + 0.5)) / IMG - 1.0
    turns = as_column(coords[0:1, :]) * gauss_ref[0:1, :] + as_column(coords[1:2, :]) * gauss_ref[1:2, :]
    sin_p, cos_p = sin_cos_turns(turns)
    prompt = jnp.concatenate([sin_p, cos_p], axis=1) + prompt_ref[...]
    start = jnp.concatenate([jnp.broadcast_to(mask_ref[...], (slots, width)), prompt], axis=0)
    weights[0].wait()
    qkv = weight_dot(start, sa_qkv_ref[...])
    q, k, v = qkv[:, :width], qkv[:, width : 2 * width], qkv[:, 2 * width :]
    k_gap = k[slots:] - k[:slots]
    v_gap = v[slots:] - v[:slots]
    self_width = width // HEADS
    i = lax.broadcasted_iota(jnp.int32, (width, width), 0) // self_width
    j = lax.broadcasted_iota(jnp.int32, (width, width), 1) // self_width
    same = jnp.where(i == j, 1.0, 0.0).astype(BF16)
    gap = weight_dot(q * jnp.concatenate([k_gap, k_gap], axis=0), same) / math.sqrt(self_width)
    second = jax.nn.sigmoid(gap)
    joined = jnp.concatenate([v[:slots], v[:slots]], axis=0) + second * jnp.concatenate([v_gap, v_gap], axis=0)
    weights[1].wait()
    queries = layer_norm(weight_dot(joined, sa_out_ref[...]), gains_ref[0:1, :])
    weights[2].wait()
    cross_q = rounded(weight_dot(queries + start, t2i_ref[:, :inner]))
    scale = math.log2(math.e) / math.sqrt(inner // HEADS)
    aq_ref[...] = (dot_t(by_head(cross_q).astype(BF16), t2i_ref[:, inner : 2 * inner]) * scale).astype(BF16)

    table_ref[0] = sin_y
    table_ref[1] = cos_y
    start_ref[...] = start
    queries_ref[...] = queries

    for y in range(side):
        if y * side % step == 0:
            cell_copies[y * side // step].wait()
        rows = slice(y * side, (y + 1) * side)
        e = emb_ref[rows, :].astype(F32)
        sy, cy = table_ref[0, y : y + 1, :], table_ref[1, y : y + 1, :]
        e1, e2 = e[:, :half], e[:, half:]
        keys_ref[rows, :half] = (e1 + (sin_x * cy + cos_x * sy)).astype(BF16)
        keys_ref[rows, half:] = (e2 + (cos_x * cy - sin_x * sy)).astype(BF16)

    pairs = HEADS * tokens

    def scores(at):
        return dot_t(aq_ref[...], keys_ref[pl.ds(at, SCORE_CELLS), :])

    def probabilities(at, s):
        for r0 in range(0, pairs, 16):
            rows = slice(r0, r0 + 16)
            top = top_ref[rows, :]
            total = sum_ref[rows, :]
            for k0 in range(0, SCORE_CELLS, LANES):
                p = jnp.exp2(s[rows, k0 : k0 + LANES] - top)
                total = total + p
                prob_ref[rows, pl.ds(pl.multiple_of(at + k0, LANES), LANES)] = p.astype(BF16)
            sum_ref[rows, :] = total

    def prob_step(c, carry):
        at = pl.multiple_of(c * SCORE_CELLS, SCORE_CELLS)
        probabilities(at, scores(at))
        return carry

    sum_ref[...] = jnp.zeros_like(sum_ref)
    first = scores(0)
    top_ref[...] = jnp.broadcast_to(jnp.max(first, axis=1, keepdims=True), top_ref.shape)
    probabilities(0, first)
    lax.fori_loop(1, cells // SCORE_CELLS, prob_step, 0)

    @pl.when(jnp.logical_not(jnp.max(sum_ref[...]) < LARGE_SUM))
    def _():
        top_ref[...] = jnp.full(top_ref.shape, -jnp.inf, F32)

        def top_step(c, carry):
            s = scores(pl.multiple_of(c * SCORE_CELLS, SCORE_CELLS))
            for k0 in range(0, SCORE_CELLS, LANES):
                top_ref[...] = jnp.maximum(top_ref[...], s[:, k0 : k0 + LANES])
            return carry

        lax.fori_loop(0, cells // SCORE_CELLS, top_step, 0)
        top_ref[...] = jnp.broadcast_to(jnp.max(top_ref[...], axis=1, keepdims=True), top_ref.shape)
        sum_ref[...] = jnp.zeros_like(sum_ref)
        lax.fori_loop(0, cells // SCORE_CELLS, prob_step, 0)

    @pl.when(count > 0)
    def _():
        mean_cell = dot(prob_ref[...], emb_ref[...]) / jnp.sum(sum_ref[...], axis=1, keepdims=True)
        head_out = dot(mean_cell.astype(BF16), t2i_ref[:, 2 * inner :])
        lane = lax.broadcasted_iota(jnp.int32, (tokens, inner), 1) // (inner // HEADS)
        cross_out = jnp.zeros((tokens, inner), F32)
        for h in range(HEADS):
            cross_out = jnp.where(lane == h, head_out[h * tokens : (h + 1) * tokens], cross_out)
        cross_ref[...] = cross_out

    @pl.when(count > 0)
    def _():
        for copy in weights[3:]:
            copy.wait()
        queries = layer_norm(queries_ref[...] + weight_dot(cross_ref[...], t2i_out_ref[...]), gains_ref[1:2, :])
        hidden = jnp.maximum(dot(queries.astype(BF16), up_ref[...]), 0.0)
        queries = layer_norm(queries + dot(hidden.astype(BF16), down_ref[...]), gains_ref[2:3, :])
        start = start_ref[...]
        back_k = rounded(weight_dot(queries + start, i2t_ref[:, inner : 2 * inner]))
        back_v = rounded(weight_dot(queries, i2t_ref[:, 2 * inner :]))
        hyper = rounded(weight_dot(jnp.maximum(weight_dot(queries[:slots], hyper_ref[0]), 0.0), hyper_ref[1]))
        back_ref[0] = back_k
        back_ref[1] = back_v
        hyper_out[...] = hyper

    group = slots // GROUPS
    heads = HEADS * group
    lines = heads + 2 * group
    blank = width - heads

    @pl.when(count > 0)
    def _():
        back_k, back_v, hyper = back_ref[0], back_ref[1], hyper_out[...]
        key_gap = back_k[:slots] - back_k[slots:]
        gap_scale = 0.5 / math.sqrt(inner // HEADS)
        spread = 0.5 * (back_v[:slots] - back_v[slots:])
        middle = 0.5 * (back_v[:slots] + back_v[slots:])
        b_all = rounded(centred_rows(weight_dot(middle, i2t_out_ref[...])))
        g_all = rounded(centred_rows(hyper * gains_ref[3:4, :]))
        zeros = jnp.zeros((blank, width), BF16)
        r = lax.broadcasted_iota(jnp.int32, (lines, width), 0)
        c = lax.broadcasted_iota(jnp.int32, (lines, width), 1)
        own_slot = jnp.logical_and(r % group == c % group, c < heads)
        for n in range(GROUPS):
            of = slice(n * group, (n + 1) * group)
            gap_ref[n * heads : (n + 1) * heads, :] = (
                dot_t(by_head(key_gap[of]).astype(BF16), i2t_ref[:, :inner]) * gap_scale
            ).astype(BF16)
            u = rounded(centred_rows(dot(by_head(spread[of]).astype(BF16), i2t_out_ref[...])))
            b, g = b_all[of], g_all[of]
            left = jnp.concatenate([u, 2.0 * b, g], axis=0).astype(BF16)
            right = jnp.concatenate([u.astype(BF16), zeros], axis=0)
            constant = jnp.concatenate(
                [
                    jnp.zeros((heads, 1), F32),
                    jnp.sum(b * b, axis=1, keepdims=True),
                    jnp.sum(b * g, axis=1, keepdims=True),
                ],
                axis=0,
            )
            high = rounded(constant)
            mix = jnp.where(own_slot, dot_t(left, right), 0.0)
            mix = jnp.where(c == heads, high, jnp.where(c == heads + 1, constant - high, mix))
            mix_ref[n] = mix.astype(BF16)
            row_ref[n * lines : (n + 1) * lines, :] = jnp.concatenate([2.0 * u, 2.0 * b, g], axis=0).astype(BF16)

    ones = jnp.ones((16, width), BF16)
    row_ref[GROUPS * lines :, :] = ones
    t_ref[:, heads:, :] = jnp.ones((GROUPS, blank, cells), BF16)

    out_copies = []
    for at in range(0, cells, IMAGE_CELLS):
        here = slice(at, at + IMAGE_CELLS)
        t = jnp.tanh(dot_t(gap_ref[...], keys_ref[here, :])).astype(BF16)
        for n in range(GROUPS):
            t_ref[n, :heads, here] = t[n * heads : (n + 1) * heads]
        cell_part = dot_t(row_ref[...], emb_ref[here, :])
        sums = cell_part[GROUPS * lines : GROUPS * lines + 8]
        e = emb_ref[here, :].astype(F32)
        squares = jnp.concatenate(halves(e[:, :half] * e[:, :half] + e[:, half:] * e[:, half:]), axis=1)
        own = dot_t(ones, squares)[:8] - sums * sums * (1.0 / width)
        logits = []
        for n in range(GROUPS):
            line = cell_part[n * lines : (n + 1) * lines] + dot(mix_ref[n], t_ref[n, :, here])
            t32 = t[n * heads : (n + 1) * heads].astype(F32)
            var = line[heads : heads + group] + jnp.concatenate([own] * (group // 8), axis=0)
            for h in range(HEADS):
                var = var + t32[h * group : (h + 1) * group] * line[h * group : (h + 1) * group]
            var = jnp.maximum(var, 0.0)
            logits.append(line[heads + group :] * lax.rsqrt(var + EPS * width))
        logit = rounded(jnp.concatenate(logits, axis=0))
        live = lax.broadcasted_iota(jnp.int32, logit.shape, 0) < count
        masked = jnp.where(live, logit, 0.0)
        logits_ref[:, here] = masked.astype(BF16)
        out_copies.append(pltpu.make_async_copy(logits_ref.at[:, here], logits_hbm.at[:, here], out_sem.at[at // IMAGE_CELLS]))
        out_copies[-1].start()
        cover = jnp.sum(jnp.where(live, jax.nn.sigmoid(masked), 0.0), axis=0, keepdims=True)
        for k0 in range(0, IMAGE_CELLS, LANES):
            cov_ref[(at + k0) // LANES : (at + k0) // LANES + 1, :] = cover[:, k0 : k0 + LANES]
    out_copies.append(pltpu.make_async_copy(cov_ref, cov_hbm, cov_sem))
    out_copies[-1].start()
    for copy in out_copies:
        copy.wait()


def seam_kernel(n, cov_hbm, left_hbm, right_hbm, zero_ref, send_sem, recv_sem, zero_sem):
    me = lax.axis_index("col")
    has_left, has_right = me > 0, me < n - 1
    barrier = pltpu.get_barrier_semaphore()
    mesh_id = pl.DeviceIdType.MESH

    def to_left():
        return pltpu.make_async_remote_copy(
            src_ref=cov_hbm,
            dst_ref=right_hbm,
            send_sem=send_sem.at[0],
            recv_sem=recv_sem.at[0],
            device_id={"col": me - 1},
            device_id_type=mesh_id,
        )

    def to_right():
        return pltpu.make_async_remote_copy(
            src_ref=cov_hbm,
            dst_ref=left_hbm,
            send_sem=send_sem.at[1],
            recv_sem=recv_sem.at[1],
            device_id={"col": me + 1},
            device_id_type=mesh_id,
        )

    @pl.when(has_left)
    def _():
        pl.semaphore_signal(barrier, inc=1, device_id={"col": me - 1}, device_id_type=mesh_id)

    @pl.when(has_right)
    def _():
        pl.semaphore_signal(barrier, inc=1, device_id={"col": me + 1}, device_id_type=mesh_id)

    pl.semaphore_wait(barrier, has_left.astype(jnp.int32) + has_right.astype(jnp.int32))

    @pl.when(has_left)
    def _():
        to_left().start()

    @pl.when(has_right)
    def _():
        to_right().start()

    @pl.when(jnp.logical_not(has_left))
    def _():
        zero_ref[...] = jnp.zeros_like(zero_ref)
        copy = pltpu.make_async_copy(zero_ref, left_hbm, zero_sem)
        copy.start()
        copy.wait()

    @pl.when(jnp.logical_not(has_right))
    def _():
        zero_ref[...] = jnp.zeros_like(zero_ref)
        copy = pltpu.make_async_copy(zero_ref, right_hbm, zero_sem)
        copy.start()
        copy.wait()

    @pl.when(has_right)
    def _():
        to_right().wait_send()
        to_left().wait_recv()

    @pl.when(has_left)
    def _():
        to_left().wait_send()
        to_right().wait_recv()


def tile_call(counts, emb, points, gauss, prompt, mask, sa_qkv, sa_out, t2i, t2i_out, up, down, i2t, i2t_out, hyper, gains):
    cells, width = emb.shape
    slots = points.shape[1]
    rows = 2 * slots * HEADS
    heads = HEADS * slots // GROUPS
    lines = heads + 2 * slots // GROUPS
    vmem = pl.BlockSpec(memory_space=pltpu.VMEM)
    hbm = pl.BlockSpec(memory_space=pl.ANY)
    large = [emb, sa_qkv, sa_out, t2i, t2i_out, up, down, i2t, i2t_out, hyper]
    return pl.pallas_call(
        tile_kernel,
        out_shape=(
            jax.ShapeDtypeStruct((slots, cells), BF16),
            jax.ShapeDtypeStruct((cells // LANES, LANES), F32),
        ),
        in_specs=[pl.BlockSpec(memory_space=pltpu.SMEM)] + [vmem] * 5 + [hbm] * len(large),
        out_specs=(hbm, hbm),
        scratch_shapes=[pltpu.VMEM(a.shape, a.dtype) for a in large]
        + [
            pltpu.VMEM((slots, cells), BF16),
            pltpu.VMEM((cells, width), BF16),
            pltpu.VMEM((rows, cells), BF16),
            pltpu.VMEM((rows, width), BF16),
            pltpu.VMEM((rows, LANES), F32),
            pltpu.VMEM((rows, LANES), F32),
            pltpu.VMEM((2 * slots, width), F32),
            pltpu.VMEM((2 * slots, width), F32),
            pltpu.VMEM((2 * slots, t2i.shape[1] // 3), F32),
            pltpu.VMEM((2, 2 * slots, t2i.shape[1] // 3), F32),
            pltpu.VMEM((slots, width), F32),
            pltpu.VMEM((GROUPS * heads, width), BF16),
            pltpu.VMEM((GROUPS * lines + 16, width), BF16),
            pltpu.VMEM((GROUPS, lines, width), BF16),
            pltpu.VMEM((GROUPS, width, cells), BF16),
            pltpu.VMEM((2, math.isqrt(cells), width // 2), F32),
            pltpu.SemaphoreType.DMA((len(large) - 1,)),
            pltpu.SemaphoreType.DMA((EMB_COPIES,)),
            pltpu.SemaphoreType.DMA((cells // IMAGE_CELLS,)),
            pltpu.VMEM((cells // LANES, LANES), F32),
            pltpu.SemaphoreType.DMA(()),
        ],
        compiler_params=pltpu.CompilerParams(vmem_limit_bytes=58 * 2**20),
        name="tile",
    )(counts, points, gauss, prompt, mask, gains, *large)


def seam_call(cov, n):
    hbm = pl.BlockSpec(memory_space=pl.ANY)
    return pl.pallas_call(
        functools.partial(seam_kernel, n),
        out_shape=(jax.ShapeDtypeStruct(cov.shape, F32), jax.ShapeDtypeStruct(cov.shape, F32)),
        in_specs=[hbm],
        out_specs=(hbm, hbm),
        scratch_shapes=[
            pltpu.VMEM(cov.shape, F32),
            pltpu.SemaphoreType.DMA((2,)),
            pltpu.SemaphoreType.DMA((2,)),
            pltpu.SemaphoreType.DMA(()),
        ],
        compiler_params=pltpu.CompilerParams(collective_id=0, has_side_effects=True),
        name="seam",
    )(cov)


def blend_kernel(left_ref, cov_ref, right_ref, out_ref):
    side = out_ref.shape[0]
    left, cov, right = left_ref[...], cov_ref[...], right_ref[...]
    x = lax.broadcasted_iota(jnp.int32, cov.shape, 1) % side
    total = (SEAM + 1.0) * cov
    for d in range(1, SEAM + 1):
        after = jnp.where(x < side - d, pltpu.roll(cov, LANES - d, 1), pltpu.roll(right, side - d, 1))
        before = jnp.where(x >= d, pltpu.roll(cov, d, 1), pltpu.roll(left, side + d, 1))
        total = total + (SEAM + 1.0 - d) * (after + before)
    total = total * (1.0 / (SEAM + 1) ** 2)
    out_ref[pl.ds(0, side // 2, stride=2), :] = total[:, :side]
    out_ref[pl.ds(1, side // 2, stride=2), :] = total[:, side:]


def blend(left, cov, right, side):
    vmem = pl.BlockSpec(memory_space=pltpu.VMEM)
    return pl.pallas_call(
        blend_kernel,
        out_shape=jax.ShapeDtypeStruct((side, side), F32),
        in_specs=[vmem] * 3,
        out_specs=vmem,
        name="blend",
    )(left, cov, right)


def shards(
    embedding,
    counts,
    points,
    pe_gauss,
    point_embed,
    mask_token,
    sa_qkv,
    sa_out,
    t2i_qkv,
    t2i_out,
    mlp_up,
    mlp_down,
    i2t_qkv,
    i2t_out,
    hyper_w,
    ln_gains,
):
    side, _, width = embedding.shape
    logits, cov = tile_call(
        counts,
        embedding.reshape(side * side, width),
        points[0, 0],
        pe_gauss,
        point_embed.reshape(1, width),
        mask_token.reshape(1, width),
        sa_qkv,
        sa_out,
        t2i_qkv,
        t2i_out,
        mlp_up,
        mlp_down,
        i2t_qkv,
        i2t_out,
        hyper_w,
        ln_gains,
    )
    left, right = seam_call(cov, lax.axis_size("col"))
    blended = blend(left, cov, right, side)
    return logits.reshape(1, 1, *logits.shape), blended


def solution(mesh):
    whole = [P()] * 13
    return jax.shard_map(
        shards,
        mesh=mesh,
        in_specs=(P("row", "col", None), P("col", None), P("row", "col", None, None), *whole),
        out_specs=(P("row", "col", None, None), P("row", "col")),
        check_vma=False,
    )
```

```python
import functools
import math

import jax
import jax.numpy as jnp
import numpy as np
from jax import lax
from jax.experimental import pallas as pl
from jax.experimental.pallas import tpu as pltpu
from jax.sharding import PartitionSpec as P

HEADS = 8
SEAM = 4
IMG = 1024
EPS = 1e-05
F32 = jnp.float32
BF16 = jnp.bfloat16
LANES = 128
GROUPS = 2
EMB_COPIES = 4
SCORE_CELLS = 1024
LARGE_SUM = 2.0**100
IMAGE_CELLS = 512


def turn_polynomials():
    z = np.linspace(0.0, 0.25, 4001)[1:]
    r = np.sqrt(z)
    fit = np.polynomial.chebyshev.Chebyshev.fit
    power = lambda c: [float(v) for v in c.convert(kind=np.polynomial.Polynomial, domain=[-1, 1]).coef]
    return (
        power(fit(z, np.sin(2 * math.pi * r) / r, 8, domain=[0.0, 0.25])),
        power(fit(z, np.cos(2 * math.pi * r), 8, domain=[0.0, 0.25])),
    )


SIN_COEF, COS_COEF = turn_polynomials()


def sin_cos_turns(turns):
    r = turns - jnp.floor(turns + 0.5)
    z = r * r
    s = jnp.full_like(z, SIN_COEF[-1])
    c = jnp.full_like(z, COS_COEF[-1])
    for a, b in zip(SIN_COEF[-2::-1], COS_COEF[-2::-1]):
        s = s * z + a
        c = c * z + b
    return s * r, c


def dot(a, b):
    return lax.dot_general(a, b, (((1,), (0,)), ((), ())), preferred_element_type=F32)


def dot_t(a, b):
    return lax.dot_general(a, b, (((1,), (1,)), ((), ())), preferred_element_type=F32)


def halves(values):
    high = values.astype(BF16)
    return high, (values - high.astype(F32)).astype(BF16)


def weight_dot(values, weight):
    rows = values.shape[0]
    both = dot(jnp.concatenate(halves(values), axis=0), weight)
    return both[:rows] + both[rows:]


def layer_norm(values, gain):
    centred = values - jnp.mean(values, axis=-1, keepdims=True)
    var = jnp.mean(centred * centred, axis=-1, keepdims=True)
    return centred * lax.rsqrt(var + EPS) * gain


def rounded(values):
    return values.astype(BF16).astype(F32)


def by_head(values):
    lane = lax.broadcasted_iota(jnp.int32, values.shape, 1) // (values.shape[1] // HEADS)
    return jnp.concatenate([jnp.where(lane == h, values, 0.0) for h in range(HEADS)], axis=0)


def centred_rows(values):
    return values - jnp.mean(values, axis=-1, keepdims=True)


def as_column(row):
    n = row.shape[1]
    i = lax.broadcasted_iota(jnp.int32, (n, n), 0)
    j = lax.broadcasted_iota(jnp.int32, (n, n), 1)
    return jnp.sum(jnp.where(i == j, jnp.broadcast_to(row, (n, n)), 0.0), axis=1, keepdims=True)


def tile_kernel(
    counts_ref,
    points_ref,
    gauss_ref,
    prompt_ref,
    mask_ref,
    gains_ref,
    emb_hbm,
    sa_qkv_hbm,
    sa_out_hbm,
    t2i_hbm,
    t2i_out_hbm,
    up_hbm,
    down_hbm,
    i2t_hbm,
    i2t_out_hbm,
    hyper_hbm,
    logits_hbm,
    cov_hbm,
    emb_ref,
    sa_qkv_ref,
    sa_out_ref,
    t2i_ref,
    t2i_out_ref,
    up_ref,
    down_ref,
    i2t_ref,
    i2t_out_ref,
    hyper_ref,
    logits_ref,
    keys_ref,
    prob_ref,
    aq_ref,
    top_ref,
    sum_ref,
    start_ref,
    queries_ref,
    cross_ref,
    back_ref,
    hyper_out,
    gap_ref,
    row_ref,
    mix_ref,
    t_ref,
    table_ref,
    in_sem,
    emb_sem,
    out_sem,
    cov_ref,
    cov_sem,
):
    cells, width = emb_ref.shape
    slots = points_ref.shape[1]
    tokens = 2 * slots
    half = width // 2
    inner = t2i_ref.shape[1] // 3
    side = math.isqrt(cells)
    count = counts_ref[0, lax.axis_index("row")]

    weights = [
        pltpu.make_async_copy(source, target, in_sem.at[i])
        for i, (source, target) in enumerate(
            [
                (sa_qkv_hbm, sa_qkv_ref),
                (sa_out_hbm, sa_out_ref),
                (t2i_hbm, t2i_ref),
                (t2i_out_hbm, t2i_out_ref),
                (up_hbm, up_ref),
                (down_hbm, down_ref),
                (i2t_hbm, i2t_ref),
                (hyper_hbm, hyper_ref),
                (i2t_out_hbm, i2t_out_ref),
            ]
        )
    ]
    step = cells // EMB_COPIES
    cell_copies = [
        pltpu.make_async_copy(emb_hbm.at[pl.ds(i * step, step)], emb_ref.at[pl.ds(i * step, step)], emb_sem.at[i])
        for i in range(EMB_COPIES)
    ]
    for copy in weights[:3] + cell_copies + weights[3:]:
        copy.start()

    steps = (2.0 * (lax.broadcasted_iota(jnp.int32, (side, half), 0).astype(F32) + 0.5)) / side - 1.0
    sin_x, cos_x = sin_cos_turns(steps * gauss_ref[0:1, :])
    sin_y, cos_y = sin_cos_turns(steps * gauss_ref[1:2, :])

    coords = (2.0 * (points_ref[...].astype(F32) + 0.5)) / IMG - 1.0
    turns = as_column(coords[0:1, :]) * gauss_ref[0:1, :] + as_column(coords[1:2, :]) * gauss_ref[1:2, :]
    sin_p, cos_p = sin_cos_turns(turns)
    prompt = jnp.concatenate([sin_p, cos_p], axis=1) + prompt_ref[...]
    start = jnp.concatenate([jnp.broadcast_to(mask_ref[...], (slots, width)), prompt], axis=0)
    weights[0].wait()
    qkv = weight_dot(start, sa_qkv_ref[...])
    q, k, v = qkv[:, :width], qkv[:, width : 2 * width], qkv[:, 2 * width :]
    k_gap = k[slots:] - k[:slots]
    v_gap = v[slots:] - v[:slots]
    self_width = width // HEADS
    i = lax.broadcasted_iota(jnp.int32, (width, width), 0) // self_width
    j = lax.broadcasted_iota(jnp.int32, (width, width), 1) // self_width
    same = jnp.where(i == j, 1.0, 0.0).astype(BF16)
    gap = weight_dot(q * jnp.concatenate([k_gap, k_gap], axis=0), same) / math.sqrt(self_width)
    second = jax.nn.sigmoid(gap)
    joined = jnp.concatenate([v[:slots], v[:slots]], axis=0) + second * jnp.concatenate([v_gap, v_gap], axis=0)
    weights[1].wait()
    queries = layer_norm(weight_dot(joined, sa_out_ref[...]), gains_ref[0:1, :])
    weights[2].wait()
    cross_q = rounded(weight_dot(queries + start, t2i_ref[:, :inner]))
    scale = math.log2(math.e) / math.sqrt(inner // HEADS)
    aq_ref[...] = (dot_t(by_head(cross_q).astype(BF16), t2i_ref[:, inner : 2 * inner]) * scale).astype(BF16)

    table_ref[0] = sin_y
    table_ref[1] = cos_y
    start_ref[...] = start
    queries_ref[...] = queries

    for y in range(side):
        if y * side % step == 0:
            cell_copies[y * side // step].wait()
        rows = slice(y * side, (y + 1) * side)
        e = emb_ref[rows, :].astype(F32)
        sy, cy = table_ref[0, y : y + 1, :], table_ref[1, y : y + 1, :]
        e1, e2 = e[:, :half], e[:, half:]
        keys_ref[rows, :half] = (e1 + (sin_x * cy + cos_x * sy)).astype(BF16)
        keys_ref[rows, half:] = (e2 + (cos_x * cy - sin_x * sy)).astype(BF16)

    pairs = HEADS * tokens

    def scores(at):
        return dot_t(aq_ref[...], keys_ref[pl.ds(at, SCORE_CELLS), :])

    def probabilities(at, s):
        for r0 in range(0, pairs, 16):
            rows = slice(r0, r0 + 16)
            top = top_ref[rows, :]
            total = sum_ref[rows, :]
            for k0 in range(0, SCORE_CELLS, LANES):
                p = jnp.exp2(s[rows, k0 : k0 + LANES] - top)
                total = total + p
                prob_ref[rows, pl.ds(pl.multiple_of(at + k0, LANES), LANES)] = p.astype(BF16)
            sum_ref[rows, :] = total

    def prob_step(c, carry):
        at = pl.multiple_of(c * SCORE_CELLS, SCORE_CELLS)
        probabilities(at, scores(at))
        return carry

    sum_ref[...] = jnp.zeros_like(sum_ref)
    first = scores(0)
    top_ref[...] = jnp.broadcast_to(jnp.max(first, axis=1, keepdims=True), top_ref.shape)
    probabilities(0, first)
    lax.fori_loop(1, cells // SCORE_CELLS, prob_step, 0)

    @pl.when(jnp.logical_not(jnp.max(sum_ref[...]) < LARGE_SUM))
    def _():
        top_ref[...] = jnp.full(top_ref.shape, -jnp.inf, F32)

        def top_step(c, carry):
            s = scores(pl.multiple_of(c * SCORE_CELLS, SCORE_CELLS))
            for k0 in range(0, SCORE_CELLS, LANES):
                top_ref[...] = jnp.maximum(top_ref[...], s[:, k0 : k0 + LANES])
            return carry

        lax.fori_loop(0, cells // SCORE_CELLS, top_step, 0)
        top_ref[...] = jnp.broadcast_to(jnp.max(top_ref[...], axis=1, keepdims=True), top_ref.shape)
        sum_ref[...] = jnp.zeros_like(sum_ref)
        lax.fori_loop(0, cells // SCORE_CELLS, prob_step, 0)

    @pl.when(count > 0)
    def _():
        mean_cell = dot(prob_ref[...], emb_ref[...]) / jnp.sum(sum_ref[...], axis=1, keepdims=True)
        head_out = dot(mean_cell.astype(BF16), t2i_ref[:, 2 * inner :])
        lane = lax.broadcasted_iota(jnp.int32, (tokens, inner), 1) // (inner // HEADS)
        cross_out = jnp.zeros((tokens, inner), F32)
        for h in range(HEADS):
            cross_out = jnp.where(lane == h, head_out[h * tokens : (h + 1) * tokens], cross_out)
        cross_ref[...] = cross_out

    @pl.when(count > 0)
    def _():
        for copy in weights[3:]:
            copy.wait()
        queries = layer_norm(queries_ref[...] + weight_dot(cross_ref[...], t2i_out_ref[...]), gains_ref[1:2, :])
        hidden = jnp.maximum(dot(queries.astype(BF16), up_ref[...]), 0.0)
        queries = layer_norm(queries + dot(hidden.astype(BF16), down_ref[...]), gains_ref[2:3, :])
        start = start_ref[...]
        back_k = rounded(weight_dot(queries + start, i2t_ref[:, inner : 2 * inner]))
        back_v = rounded(weight_dot(queries, i2t_ref[:, 2 * inner :]))
        hyper = rounded(weight_dot(jnp.maximum(weight_dot(queries[:slots], hyper_ref[0]), 0.0), hyper_ref[1]))
        back_ref[0] = back_k
        back_ref[1] = back_v
        hyper_out[...] = hyper

    group = slots // GROUPS
    heads = HEADS * group
    lines = heads + 2 * group
    blank = width - heads

    @pl.when(count > 0)
    def _():
        back_k, back_v, hyper = back_ref[0], back_ref[1], hyper_out[...]
        key_gap = back_k[:slots] - back_k[slots:]
        gap_scale = 0.5 / math.sqrt(inner // HEADS)
        spread = 0.5 * (back_v[:slots] - back_v[slots:])
        middle = 0.5 * (back_v[:slots] + back_v[slots:])
        b_all = rounded(centred_rows(weight_dot(middle, i2t_out_ref[...])))
        g_all = rounded(centred_rows(hyper * gains_ref[3:4, :]))
        zeros = jnp.zeros((blank, width), BF16)
        r = lax.broadcasted_iota(jnp.int32, (lines, width), 0)
        c = lax.broadcasted_iota(jnp.int32, (lines, width), 1)
        own_slot = jnp.logical_and(r % group == c % group, c < heads)
        for n in range(GROUPS):
            of = slice(n * group, (n + 1) * group)
            gap_ref[n * heads : (n + 1) * heads, :] = (
                dot_t(by_head(key_gap[of]).astype(BF16), i2t_ref[:, :inner]) * gap_scale
            ).astype(BF16)
            u = rounded(centred_rows(dot(by_head(spread[of]).astype(BF16), i2t_out_ref[...])))
            b, g = b_all[of], g_all[of]
            left = jnp.concatenate([u, 2.0 * b, g], axis=0).astype(BF16)
            right = jnp.concatenate([u.astype(BF16), zeros], axis=0)
            constant = jnp.concatenate(
                [
                    jnp.zeros((heads, 1), F32),
                    jnp.sum(b * b, axis=1, keepdims=True),
                    jnp.sum(b * g, axis=1, keepdims=True),
                ],
                axis=0,
            )
            high = rounded(constant)
            mix = jnp.where(own_slot, dot_t(left, right), 0.0)
            mix = jnp.where(c == heads, high, jnp.where(c == heads + 1, constant - high, mix))
            mix_ref[n] = mix.astype(BF16)
            row_ref[n * lines : (n + 1) * lines, :] = jnp.concatenate([2.0 * u, 2.0 * b, g], axis=0).astype(BF16)

    ones = jnp.ones((16, width), BF16)
    row_ref[GROUPS * lines :, :] = ones
    t_ref[:, heads:, :] = jnp.ones((GROUPS, blank, cells), BF16)

    out_copies = []

    def two_token(at):
        here = slice(at, at + IMAGE_CELLS)
        t = jnp.tanh(dot_t(gap_ref[...], keys_ref[here, :])).astype(BF16)
        for n in range(GROUPS):
            t_ref[n, :heads, here] = t[n * heads : (n + 1) * heads]

    two_token(0)
    for at in range(0, cells, IMAGE_CELLS):
        here = slice(at, at + IMAGE_CELLS)
        if at + IMAGE_CELLS < cells:
            two_token(at + IMAGE_CELLS)
        cell_part = dot_t(row_ref[...], emb_ref[here, :])
        sums = cell_part[GROUPS * lines : GROUPS * lines + 8]
        e = emb_ref[here, :].astype(F32)
        squares = jnp.concatenate(halves(e[:, :half] * e[:, :half] + e[:, half:] * e[:, half:]), axis=1)
        own = dot_t(ones, squares)[:8] - sums * sums * (1.0 / width)
        logits = []
        for n in range(GROUPS):
            line = cell_part[n * lines : (n + 1) * lines] + dot(mix_ref[n], t_ref[n, :, here])
            t32 = t_ref[n, :heads, here].astype(F32)
            var = line[heads : heads + group] + jnp.concatenate([own] * (group // 8), axis=0)
            for h in range(HEADS):
                var = var + t32[h * group : (h + 1) * group] * line[h * group : (h + 1) * group]
            var = jnp.maximum(var, 0.0)
            logits.append(line[heads + group :] * lax.rsqrt(var + EPS * width))
        logit = rounded(jnp.concatenate(logits, axis=0))
        live = lax.broadcasted_iota(jnp.int32, logit.shape, 0) < count
        masked = jnp.where(live, logit, 0.0)
        logits_ref[:, here] = masked.astype(BF16)
        out_copies.append(pltpu.make_async_copy(logits_ref.at[:, here], logits_hbm.at[:, here], out_sem.at[at // IMAGE_CELLS]))
        out_copies[-1].start()
        cover = jnp.sum(jnp.where(live, jax.nn.sigmoid(masked), 0.0), axis=0, keepdims=True)
        for k0 in range(0, IMAGE_CELLS, LANES):
            cov_ref[(at + k0) // LANES : (at + k0) // LANES + 1, :] = cover[:, k0 : k0 + LANES]
    out_copies.append(pltpu.make_async_copy(cov_ref, cov_hbm, cov_sem))
    out_copies[-1].start()
    for copy in out_copies:
        copy.wait()


def seam_kernel(n, cov_hbm, left_hbm, right_hbm, zero_ref, send_sem, recv_sem, zero_sem):
    me = lax.axis_index("col")
    has_left, has_right = me > 0, me < n - 1
    barrier = pltpu.get_barrier_semaphore()
    mesh_id = pl.DeviceIdType.MESH

    def to_left():
        return pltpu.make_async_remote_copy(
            src_ref=cov_hbm,
            dst_ref=right_hbm,
            send_sem=send_sem.at[0],
            recv_sem=recv_sem.at[0],
            device_id={"col": me - 1},
            device_id_type=mesh_id,
        )

    def to_right():
        return pltpu.make_async_remote_copy(
            src_ref=cov_hbm,
            dst_ref=left_hbm,
            send_sem=send_sem.at[1],
            recv_sem=recv_sem.at[1],
            device_id={"col": me + 1},
            device_id_type=mesh_id,
        )

    @pl.when(has_left)
    def _():
        pl.semaphore_signal(barrier, inc=1, device_id={"col": me - 1}, device_id_type=mesh_id)

    @pl.when(has_right)
    def _():
        pl.semaphore_signal(barrier, inc=1, device_id={"col": me + 1}, device_id_type=mesh_id)

    pl.semaphore_wait(barrier, has_left.astype(jnp.int32) + has_right.astype(jnp.int32))

    @pl.when(has_left)
    def _():
        to_left().start()

    @pl.when(has_right)
    def _():
        to_right().start()

    @pl.when(jnp.logical_not(has_left))
    def _():
        zero_ref[...] = jnp.zeros_like(zero_ref)
        copy = pltpu.make_async_copy(zero_ref, left_hbm, zero_sem)
        copy.start()
        copy.wait()

    @pl.when(jnp.logical_not(has_right))
    def _():
        zero_ref[...] = jnp.zeros_like(zero_ref)
        copy = pltpu.make_async_copy(zero_ref, right_hbm, zero_sem)
        copy.start()
        copy.wait()

    @pl.when(has_right)
    def _():
        to_right().wait_send()
        to_left().wait_recv()

    @pl.when(has_left)
    def _():
        to_left().wait_send()
        to_right().wait_recv()


def tile_call(counts, emb, points, gauss, prompt, mask, sa_qkv, sa_out, t2i, t2i_out, up, down, i2t, i2t_out, hyper, gains):
    cells, width = emb.shape
    slots = points.shape[1]
    rows = 2 * slots * HEADS
    heads = HEADS * slots // GROUPS
    lines = heads + 2 * slots // GROUPS
    vmem = pl.BlockSpec(memory_space=pltpu.VMEM)
    hbm = pl.BlockSpec(memory_space=pl.ANY)
    large = [emb, sa_qkv, sa_out, t2i, t2i_out, up, down, i2t, i2t_out, hyper]
    return pl.pallas_call(
        tile_kernel,
        out_shape=(
            jax.ShapeDtypeStruct((slots, cells), BF16),
            jax.ShapeDtypeStruct((cells // LANES, LANES), F32),
        ),
        in_specs=[pl.BlockSpec(memory_space=pltpu.SMEM)] + [vmem] * 5 + [hbm] * len(large),
        out_specs=(hbm, hbm),
        scratch_shapes=[pltpu.VMEM(a.shape, a.dtype) for a in large]
        + [
            pltpu.VMEM((slots, cells), BF16),
            pltpu.VMEM((cells, width), BF16),
            pltpu.VMEM((rows, cells), BF16),
            pltpu.VMEM((rows, width), BF16),
            pltpu.VMEM((rows, LANES), F32),
            pltpu.VMEM((rows, LANES), F32),
            pltpu.VMEM((2 * slots, width), F32),
            pltpu.VMEM((2 * slots, width), F32),
            pltpu.VMEM((2 * slots, t2i.shape[1] // 3), F32),
            pltpu.VMEM((2, 2 * slots, t2i.shape[1] // 3), F32),
            pltpu.VMEM((slots, width), F32),
            pltpu.VMEM((GROUPS * heads, width), BF16),
            pltpu.VMEM((GROUPS * lines + 16, width), BF16),
            pltpu.VMEM((GROUPS, lines, width), BF16),
            pltpu.VMEM((GROUPS, width, cells), BF16),
            pltpu.VMEM((2, math.isqrt(cells), width // 2), F32),
            pltpu.SemaphoreType.DMA((len(large) - 1,)),
            pltpu.SemaphoreType.DMA((EMB_COPIES,)),
            pltpu.SemaphoreType.DMA((cells // IMAGE_CELLS,)),
            pltpu.VMEM((cells // LANES, LANES), F32),
            pltpu.SemaphoreType.DMA(()),
        ],
        compiler_params=pltpu.CompilerParams(vmem_limit_bytes=58 * 2**20),
        name="tile",
    )(counts, points, gauss, prompt, mask, gains, *large)


def seam_call(cov, n):
    hbm = pl.BlockSpec(memory_space=pl.ANY)
    return pl.pallas_call(
        functools.partial(seam_kernel, n),
        out_shape=(jax.ShapeDtypeStruct(cov.shape, F32), jax.ShapeDtypeStruct(cov.shape, F32)),
        in_specs=[hbm],
        out_specs=(hbm, hbm),
        scratch_shapes=[
            pltpu.VMEM(cov.shape, F32),
            pltpu.SemaphoreType.DMA((2,)),
            pltpu.SemaphoreType.DMA((2,)),
            pltpu.SemaphoreType.DMA(()),
        ],
        compiler_params=pltpu.CompilerParams(collective_id=0, has_side_effects=True),
        name="seam",
    )(cov)


def blend_kernel(left_ref, cov_ref, right_ref, out_ref):
    side = out_ref.shape[0]
    left, cov, right = left_ref[...], cov_ref[...], right_ref[...]
    x = lax.broadcasted_iota(jnp.int32, cov.shape, 1) % side
    total = (SEAM + 1.0) * cov
    for d in range(1, SEAM + 1):
        after = jnp.where(x < side - d, pltpu.roll(cov, LANES - d, 1), pltpu.roll(right, side - d, 1))
        before = jnp.where(x >= d, pltpu.roll(cov, d, 1), pltpu.roll(left, side + d, 1))
        total = total + (SEAM + 1.0 - d) * (after + before)
    total = total * (1.0 / (SEAM + 1) ** 2)
    out_ref[pl.ds(0, side // 2, stride=2), :] = total[:, :side]
    out_ref[pl.ds(1, side // 2, stride=2), :] = total[:, side:]


def blend(left, cov, right, side):
    vmem = pl.BlockSpec(memory_space=pltpu.VMEM)
    return pl.pallas_call(
        blend_kernel,
        out_shape=jax.ShapeDtypeStruct((side, side), F32),
        in_specs=[vmem] * 3,
        out_specs=vmem,
        name="blend",
    )(left, cov, right)


def shards(
    embedding,
    counts,
    points,
    pe_gauss,
    point_embed,
    mask_token,
    sa_qkv,
    sa_out,
    t2i_qkv,
    t2i_out,
    mlp_up,
    mlp_down,
    i2t_qkv,
    i2t_out,
    hyper_w,
    ln_gains,
):
    side, _, width = embedding.shape
    logits, cov = tile_call(
        counts,
        embedding.reshape(side * side, width),
        points[0, 0],
        pe_gauss,
        point_embed.reshape(1, width),
        mask_token.reshape(1, width),
        sa_qkv,
        sa_out,
        t2i_qkv,
        t2i_out,
        mlp_up,
        mlp_down,
        i2t_qkv,
        i2t_out,
        hyper_w,
        ln_gains,
    )
    left, right = seam_call(cov, lax.axis_size("col"))
    blended = blend(left, cov, right, side)
    return logits.reshape(1, 1, *logits.shape), blended


def solution(mesh):
    whole = [P()] * 13
    return jax.shard_map(
        shards,
        mesh=mesh,
        in_specs=(P("row", "col", None), P("col", None), P("row", "col", None, None), *whole),
        out_specs=(P("row", "col", None, None), P("row", "col")),
        check_vma=False,
    )
```
